128 devices in a mesh: grp: 32 (over x, y, core), exp: 4 (over z).
Axes of the slice: x: 4, y: 4, z: 4, core: 2. Of those that a mesh axis runs over, the one named last changes fastest.
Arguments:
- hidden_in: bfloat16 [16384, 7168], P(('grp', 'exp')), may hold values from -6 to 6
- weights: bfloat16 [114688, 4096], P(('grp', 'exp')), may hold values from -0.0625 to 0.0625
- gates: float32 [16384], P(('grp', 'exp')), may hold values from 0.1 to 1
- group_ids: int32 [16384], P(('grp', 'exp')), may hold values from 0 to 15, as said below
- slot_ids: int32 [16384], P(('grp', 'exp')), may hold values from 0 to 9, as said below
- out_grad: bfloat16 [16384, 4096], P(('grp', 'exp')), may hold values from -6 to 6
Outputs:
- mixed_out: bfloat16 [16384, 4096], P(('grp', 'exp'))
- hidden_grad: bfloat16 [16384, 7168], P(('grp', 'exp'))
- weight_grad: bfloat16 [114688, 4096], P(('grp', 'exp'))
- gate_grad: float32 [16384], P(('grp', 'exp'))
The draws below stay inside these ranges and needn't reach their ends.
Inputs may be any that keep to these rules, and one draw needn't show every extreme that they name: `group_ids`: on each device at most 10 of its 128 tokens name one group, and on every device some group is named by exactly 10 tokens. `slot_ids`: tokens of one device that name the same group have distinct slots.
All inputs are finite; a program needn't handle non-finite values.
Results may differ from the reference program's by a relative error of at most 0.017.
Values may be sent and summed in bfloat16 or wider, within the bound.
A program may use at most 192 MiB of HBM per device.

```python
import jax
import jax.numpy as jnp
from jax import lax

D = 4096
FF = 7168
TOK_DEV = 128
GROUPS = 16
CAP = 10
FF_DEV = 896
TOKENS = 16384


def route_table(key):
    blocks = TOKENS // TOK_DEV
    slots_total = GROUPS * CAP

    def one_block(block_number):
        subkey = jax.random.fold_in(key, block_number)
        key_pref, key_noise, key_full, key_order = jax.random.split(subkey, 4)
        entries = jnp.arange(slots_total, dtype=jnp.int32)
        group_of = entries // CAP
        preference = jax.random.randint(key_pref, (GROUPS,), 0, 1 << 20)
        noise = jax.random.randint(key_noise, (slots_total,), 0, 1 << 20)
        full_group = jax.random.randint(key_full, (), 0, GROUPS)
        score = noise + preference[group_of] + jnp.where(group_of == full_group, 1 << 22, 0)
        chosen = jnp.argsort(-score, stable=True)[:TOK_DEV]
        chosen = jax.random.permutation(key_order, chosen)
        return ((chosen // CAP).astype(jnp.int32), (chosen % CAP).astype(jnp.int32))
    groups_drawn, slots_drawn = jax.vmap(one_block)(jnp.arange(blocks, dtype=jnp.int32))
    return (groups_drawn.reshape(-1), slots_drawn.reshape(-1))


def draw_group_ids(key, part):
    groups_drawn, slots_drawn = route_table(key)
    return groups_drawn


def draw_slot_ids(key, part):
    groups_drawn, slots_drawn = route_table(key)
    return slots_drawn


def block_scale(stream_key, shape, cuts, smallest, high):
    factor_of = 1.0
    for dim, blocks in cuts:
        heights = jax.random.uniform(jax.random.fold_in(jax.random.fold_in(stream_key, 6), dim), (blocks,), jnp.float32, smallest / len(cuts), high / len(cuts))
        factor_of = factor_of * jnp.repeat(jnp.exp(heights), shape[dim] // blocks).reshape((-1,) + (1,) * (len(shape) - 1 - dim))
    return factor_of


def gaussian(rng, extent, scale, limit, pieces=(), kind=jnp.bfloat16):
    gain = block_scale(rng, extent, pieces, -0.22, 0.18) if pieces else 1.0
    values = jax.random.normal(rng, extent, jnp.float32) * scale * gain
    return jnp.minimum(jnp.maximum(values, -limit), limit).astype(kind)


def setup_inputs(seed: int = 0) -> dict:
    splits = jax.random.split(jax.random.key(seed), 7)
    hidden_in = gaussian(splits[0], (TOKENS, FF), 1.0, 6.0, ((0, 128),))
    weights = gaussian(splits[1], (GROUPS * FF, D), FF ** -0.5, 0.0625, ((0, 128),))
    gates = jnp.clip(0.1 + 0.9 * jax.random.uniform(splits[2], (TOKENS,), jnp.float32) ** block_scale(splits[2], (TOKENS,), ((0, 128),), -0.2, 0.2), 0.1, 1.0)
    group_ids = draw_group_ids(jax.random.fold_in(splits[6], 71), 0)
    slot_ids = draw_slot_ids(jax.random.fold_in(splits[6], 71), 0)
    out_grad = gaussian(splits[5], (TOKENS, D), 1.0, 6.0, ((0, 128),))
    return {"hidden_in": hidden_in, "weights": weights, "gates": gates, "group_ids": group_ids, "slot_ids": slot_ids, "out_grad": out_grad}


def place_rows(slot_index, values):
    return jnp.zeros((GROUPS * CAP, values.shape[1]), values.dtype).at[slot_index].set(values)


def by_group(table, devices):
    width = table.shape[2]
    return table.reshape(devices, GROUPS, CAP, width).transpose(1, 0, 2, 3).reshape(GROUPS, devices * CAP, width)


def by_device(table, devices):
    width = table.shape[2]
    return table.reshape(GROUPS, devices, CAP, width).transpose(1, 0, 2, 3).reshape(devices, GROUPS * CAP, width)


def take_rows(table, slot_index):
    return table[slot_index]


def reference(hidden_in, weights, gates, group_ids, slot_ids, out_grad):
    devices = TOKENS // TOK_DEV
    shards = FF // FF_DEV
    position = (group_ids * CAP + slot_ids).astype(jnp.int32).reshape(devices, TOK_DEV)
    dispatched = by_group(jax.vmap(place_rows)(position, hidden_in.reshape(devices, TOK_DEV, FF)), devices)
    weight_blocks = weights.reshape(GROUPS, shards, FF_DEV, D)

    def expert_forward(operands):
        group_rows, group_weights = operands
        total = jnp.zeros((group_rows.shape[0], D), jnp.float32)
        for shard in range(shards):
            partial_value = jnp.dot(group_rows[:, shard * FF_DEV:(shard + 1) * FF_DEV], group_weights[shard], preferred_element_type=jnp.float32)
            total = total + partial_value.astype(jnp.bfloat16).astype(jnp.float32)
        return total.astype(jnp.bfloat16)

    expert_out = lax.map(expert_forward, (dispatched, weight_blocks))
    picked = jax.vmap(take_rows)(by_device(expert_out, devices), position).reshape(TOKENS, D).astype(jnp.float32)
    mixed_out = (gates[:, None] * picked).astype(jnp.bfloat16)
    gate_grad = jnp.sum(out_grad.astype(jnp.float32) * picked, axis=1)
    cotangent = (gates[:, None] * out_grad.astype(jnp.float32)).astype(jnp.bfloat16)
    cot_slots = by_group(jax.vmap(place_rows)(position, cotangent.reshape(devices, TOK_DEV, D)), devices)

    def expert_backward(operands):
        group_rows, group_cots, group_weights = operands
        grads = []
        for shard in range(shards):
            grads.append(lax.dot_general(group_cots, group_weights[shard], (((1,), (1,)), ((), ())), preferred_element_type=jnp.float32).astype(jnp.bfloat16))
        slot_grad = jnp.concatenate(grads, axis=1)
        group_wgrad = lax.dot_general(group_rows, group_cots, (((0,), (0,)), ((), ())), preferred_element_type=jnp.float32).astype(jnp.bfloat16)
        return slot_grad, group_wgrad

    slot_grad, weight_grad = lax.map(expert_backward, (dispatched, cot_slots, weights.reshape(GROUPS, shards, FF_DEV, D)))
    hidden_grad = jax.vmap(take_rows)(by_device(slot_grad, devices), position).reshape(TOKENS, FF)
    return mixed_out, hidden_grad, weight_grad.reshape(GROUPS * FF, D), gate_grad
```

```python
import functools

import jax
import jax.numpy as jnp
from jax import lax
from jax.experimental import pallas as pl
from jax.experimental.pallas import tpu as pltpu
from jax.sharding import PartitionSpec as P

MESH = pl.DeviceIdType.MESH
BF = jnp.bfloat16
F32 = jnp.float32
TOK, CAP = 128, 10
D, FF, FB = 4096, 7168, 896
HD, QD, XD = D // 2, D // 4, D // 8
NP, NZ = 16, 4
MAIN, EXT, ROWS = 256, 64, 320


def hops(k):
    return min(k, 4 - k)


PLANE = sorted(
    [(i, j) for i in range(4) for j in range(4) if i + j], key=lambda o: -(hops(o[0]) + hops(o[1]))
)
COLUMN = [(0, 2), (1, 2), (0, 1), (0, 3), (1, 1), (1, 3), (1, 0)]


def dot(a, b, dims=((1,), (0,))):
    return lax.dot_general(a, b, (dims, ((), ())), preferred_element_type=F32)


def dot_tn(a, b):
    return dot(a, b, ((0,), (0,)))


def dot_nt(a, b):
    return dot(a, b, ((1,), (1,)))


def one(cond):
    return jnp.where(cond, 1.0, 0.0).astype(F32).astype(BF)


def iota(shape, dim):
    return lax.broadcasted_iota(jnp.int32, shape, dim)


def mult(value, of):
    return pl.multiple_of(value, of)


def kernel(
    hid, w_hbm, gates, pos, og_hbm,
    mixed, hg, wg, gg,
    wv, h, hxr, cot, cxp, xh, sm, sx, tok, tsend, gm, gx, pa, prcv, r1, r2, ex, em, exr, hp, hpx, rm, rx, kk, kr, og,
    mt, xb, posv,
    pos_s, pos_r, hz_s, hz_r, w_sem, og_sem, t_s, t_r, cm_s, cm_r, cx_s, cx_r, hm_s, hm_r,
    ag_s, ag_r, agf_s, agf_r, sib_s, sib_r, po_s, po_r, rs_s, rs_r, ret_s, ret_r, eo_s, eo_r, k_s, k_r, hg_s, hg_r, wg_sem,
):
    g = lax.axis_index("grp")
    z = lax.axis_index("exp")
    c = lax.rem(g, 2)
    p = lax.div(g, 2)
    x = lax.div(p, 4)
    y = lax.rem(p, 4)
    nc = 1 - c
    zp = lax.rem(z + 1, 4)
    zm = lax.rem(z + 3, 4)
    zo = lax.rem(z + 2, 4)
    sib = (p * 2 + nc, z)
    up = (g, zp)
    down = (g, zm)
    blk = c * 4 + z

    def plane(i, j):
        p2 = lax.rem(x + i, 4) * 4 + lax.rem(y + j, 4)
        return p2, (p2 * 2 + c, z)

    def column(dc, dz):
        c2 = lax.rem(c + dc, 2)
        z2 = lax.rem(z + dz, 4)
        return c2, z2, (p * 2 + c2, z2)

    def remote(src, dst, ss, rs, dev):
        return pltpu.make_async_remote_copy(
            src_ref=src, dst_ref=dst, send_sem=ss, recv_sem=rs, device_id=dev, device_id_type=MESH
        )

    def local(src, dst, sem):
        return pltpu.make_async_copy(src, dst, sem)

    def drain(ref, sem):
        pltpu.make_async_copy(ref, ref, sem).wait()

    def rows(ref, start, size, of=16):
        return ref.at[pl.ds(mult(start, of), size)]

    def cols(start, size):
        return pl.ds(mult(start, 128), size)

    local(og_hbm, og, og_sem.at[0]).start()
    local(w_hbm, wv, w_sem.at[0]).start()
    posv[pl.ds(mult((z * 2 + c) * 8, 8), 8), :] = pos[...]

    barrier = pltpu.get_barrier_semaphore()
    for dc, dz in COLUMN:
        pl.semaphore_signal(barrier, inc=1, device_id=column(dc, dz)[2], device_id_type=MESH)
    for i, j in PLANE:
        pl.semaphore_signal(barrier, inc=1, device_id=plane(i, j)[1], device_id_type=MESH)
    pl.semaphore_wait(barrier, len(COLUMN) + len(PLANE))

    mine = rows(posv, (z * 2 + c) * 8, 8, 8)
    for dc, dz in COLUMN:
        remote(mine, mine, pos_s.at[0], pos_r.at[0], column(dc, dz)[2]).start()

    def send_hidden(piece, _):
        for dc, dz in COLUMN:
            c2, z2, dev = column(dc, dz)
            src = hid.at[pl.ds(mult(piece * 32, 16), 32), cols((c2 * 4 + z2) * FB, FB)]
            dst = rows(xh, (z * 2 + c) * TOK + piece * 32, 32)
            remote(src, dst, hz_s.at[0], hz_r.at[0], dev).start()
        return 0

    lax.fori_loop(0, 4, send_hidden, 0)
    local(hid.at[:, cols(blk * FB, FB)], rows(xh, (z * 2 + c) * TOK, TOK), hz_r.at[0]).start()

    eye = iota((TOK, TOK), 0) == iota((TOK, TOK), 1)
    gate = jnp.sum(jnp.where(eye, gates[...], 0.0), axis=1, keepdims=True)
    drain(og, og_sem.at[0])
    tsend[...] = (gate * og[:, cols(nc * HD, HD)].astype(F32)).astype(BF)
    remote(tsend, rows(tok, c * TOK, TOK), t_s.at[0], t_r.at[0], sib).start()
    tok[pl.ds(mult(c * TOK, 16), TOK), :] = (gate * og[:, cols(c * HD, HD)].astype(F32)).astype(BF)

    drain(rows(posv, 0, 56, 8), pos_r.at[0])

    def tables(zz, _):
        group = iota((MAIN, TOK), 0) // 16
        slot = iota((MAIN, TOK), 0) % 16
        both = posv[pl.ds(mult(zz * 16, 16), 16), :]
        first, second = both[0:1, :], both[8:9, :]
        at = pl.ds(mult(zz * MAIN, 16), MAIN)
        mt[at, 0:TOK] = one((slot < CAP) & (group * CAP + slot == first))
        mt[at, TOK : 2 * TOK] = one((slot >= CAP) & (group * CAP + slot - CAP == second))
        xb[at, :] = one(group * CAP + slot % 4 + 6 == second)
        return 0

    lax.fori_loop(0, NZ, tables, 0)
    part = (iota((MAIN, TOK), 0) // 4) % 4

    def extra_pick(zz, q):
        base = xb[pl.ds(mult(zz * MAIN, 16), MAIN), :]
        return jnp.where(part == q, base.astype(F32), 0.0).astype(BF)

    def table(zz):
        return mt[pl.ds(mult(zz * MAIN, 16), MAIN), :]

    drain(tsend, t_r.at[0])
    gm[...] = dot(table(z), tok[...]).astype(BF)
    gx[...] = sum(
        dot(extra_pick(z, q), tok[TOK : 2 * TOK, q * XD : (q + 1) * XD]) for q in range(4)
    ).astype(BF)
    own_half = cols(c * HD, HD)
    for i, j in PLANE:
        p2, dev = plane(i, j)
        here = cot.at[pl.ds(mult(z * ROWS + p * 16, 16), 16), own_half]
        remote(rows(gm, p2 * 16, 16), here, cm_s.at[0], cm_r.at[0], dev).start()
        remote(rows(gx, p2 * 16, 16), rows(cxp, p * 16, 16), cx_s.at[0], cx_r.at[0], dev).start()
    local(
        rows(gm, p * 16, 16), cot.at[pl.ds(mult(z * ROWS + p * 16, 16), 16), own_half], cm_r.at[0]
    ).start()
    local(rows(gx, p * 16, 16), rows(cxp, p * 16, 16), cx_r.at[0]).start()

    def cot_block(zz, start, size):
        return cot.at[pl.ds(mult(zz * ROWS, 16), ROWS), cols(c * HD + start, size)]

    def to_sibling(zz):
        ref = cot_block(zz, 0, HD)
        remote(ref, ref, sib_s.at[zz], sib_r.at[zz], sib).start()

    drain(cxp, cx_r.at[0])
    place = (iota((EXT, MAIN), 0) // 4 == iota((EXT, MAIN), 1) // 16) & (
        iota((EXT, MAIN), 0) % 4 == iota((EXT, MAIN), 1) % 4
    )
    for q in range(4):
        unpack = one(place & ((iota((EXT, MAIN), 1) // 4) % 4 == q))
        cot[pl.ds(mult(z * ROWS + MAIN, 16), EXT), cols(c * HD + q * XD, XD)] = dot(
            unpack, cxp[...]
        ).astype(BF)
    drain(cot.at[pl.ds(mult(z * ROWS, 16), MAIN), own_half], cm_r.at[0])
    low, high = cot_block(z, 0, QD), cot_block(z, QD, QD)
    remote(low, low, ag_s.at[0], ag_r.at[0], up).start()
    remote(high, high, ag_s.at[1], ag_r.at[1], down).start()
    remote(high, high, ag_s.at[2], ag_r.at[2], up).start()
    remote(low, low, ag_s.at[3], ag_r.at[3], down).start()
    to_sibling(z)

    drain(xh, hz_r.at[0])
    sx[...] = sum(
        dot(extra_pick(zz, zz), xh[(2 * zz + 1) * TOK : (2 * zz + 2) * TOK, :]) for zz in range(NZ)
    ).astype(BF)

    def send_slots(src, dst_start, ref, ss, rs):
        for i, j in PLANE:
            p2, dev = plane(i, j)
            remote(src(p2), rows(ref, dst_start, 16), ss, rs, dev).start()
        local(src(p), rows(ref, dst_start, 16), rs).start()

    send_slots(lambda p2: rows(sx, p2 * 16, 16), p * 16, hxr, hm_s.at[4], hm_r.at[4])

    def order(k):
        return lax.rem(z + jnp.where(k == 2, 3, jnp.where(k == 3, 0, 2 - k)), 4)

    def pick_hidden(k, _):
        zz = order(k)
        at = pl.ds(mult(zz * MAIN, 16), MAIN)
        sm[at, :] = dot(table(zz), xh[at, :]).astype(BF)
        send_slots(
            lambda p2: rows(sm, zz * MAIN + p2 * 16, 16),
            zz * ROWS + p * 16,
            h,
            hm_s.at[zz],
            hm_r.at[zz],
        )
        return 0

    lax.fori_loop(0, NZ, pick_hidden, 0)

    drain(wv, w_sem.at[0])

    def slot_grads(zz):
        at = pl.ds(mult(zz * ROWS, 16), ROWS)
        hp[at, :] = dot_nt(cot[at, :], wv[...]).astype(BF)
        send_slots(
            lambda p2: rows(hp, zz * ROWS + p2 * 16, 16),
            zz * MAIN + p * 16,
            rm,
            ret_s.at[zz],
            ret_r.at[zz],
        )

    def other_half(zz):
        return cot.at[pl.ds(mult(zz * ROWS, 16), ROWS), cols(nc * HD, HD)]

    drain(other_half(z), sib_r.at[z])
    slot_grads(z)

    mine_out = pa.at[c]
    drain(hxr, hm_r.at[4])
    swap = one(
        (iota((MAIN, MAIN), 0) // 64 == (iota((MAIN, MAIN), 1) // 4) % 4)
        & ((iota((MAIN, MAIN), 0) // 4) % 16 == iota((MAIN, MAIN), 1) // 16)
        & (iota((MAIN, MAIN), 0) % 4 == iota((MAIN, MAIN), 1) % 4)
    )
    moved = dot(swap, hxr[...]).astype(BF)
    for zz in range(NZ):
        h[zz * ROWS + MAIN : (zz + 1) * ROWS, :] = moved[zz * EXT : (zz + 1) * EXT, :]

    def add_into(zz, start, size, ref):
        def step(i, _):
            at = pl.ds(mult(zz * ROWS + i * 32, 16), 32)
            where = cols(start, size)
            mine_out[at, where] = (
                mine_out[at, where].astype(F32) + ref(i)[...].astype(F32)
            ).astype(BF)
            return 0

        lax.fori_loop(0, ROWS // 32, step, 0)

    def add_cores(zz):
        drain(prcv.at[pl.ds(mult(zz * ROWS, 16), ROWS)], po_r.at[zz])
        add_into(zz, 0, HD, lambda i: prcv.at[pl.ds(mult(zz * ROWS + i * 32, 16), 32)])

    def out_block(zz, start):
        return mine_out.at[pl.ds(mult(zz * ROWS, 16), ROWS), pl.ds(start, QD)]

    def r2_half(n, start):
        return r2.at[n, :, pl.ds(start, QD)]

    def partials(k, _):
        zz = order(k)
        at = pl.ds(mult(zz * ROWS, 16), ROWS)

        @pl.when(k == 0)
        def _():
            drain(cot_block(zm, 0, QD), ag_r.at[0])
            ref = cot_block(zm, 0, QD)
            remote(ref, ref, agf_s.at[0], agf_r.at[0], up).start()
            drain(cot_block(zp, QD, QD), ag_r.at[1])
            ref2 = cot_block(zp, QD, QD)
            remote(ref2, ref2, agf_s.at[1], agf_r.at[1], down).start()

        drain(h.at[pl.ds(mult(zz * ROWS, 16), MAIN)], hm_r.at[zz])
        rows_in = h[at, :]

        def product(half):
            def tile(j, _):
                pa[half, at, cols(j * QD, QD)] = dot(
                    rows_in, wv[:, cols(half * HD + j * QD, QD)]
                ).astype(BF)
                return 0

            lax.fori_loop(0, 2, tile, 0)

        product(nc)
        remote(
            pa.at[nc, at], prcv.at[at], po_s.at[zz], po_r.at[zz], sib
        ).start()
        product(c)

        @pl.when(k == 1)
        def _():
            add_cores(zo)
            remote(out_block(zo, 0), r1.at[0], rs_s.at[0], rs_r.at[0], up).start()
            remote(out_block(zo, QD), r1.at[1], rs_s.at[1], rs_r.at[1], down).start()

        @pl.when(k == 2)
        def _():
            add_cores(zp)
            remote(out_block(zp, QD), r2_half(0, QD), rs_s.at[2], rs_r.at[2], up).start()
            drain(cot_block(zm, QD, QD), ag_r.at[2])
            to_sibling(zm)
            drain(cot_block(zp, 0, QD), ag_r.at[3])
            to_sibling(zp)

        @pl.when(k == 3)
        def _():
            add_cores(zm)
            remote(out_block(zm, 0), r2_half(1, 0), rs_s.at[3], rs_r.at[3], down).start()

        return 0

    lax.fori_loop(0, NZ, partials, 0)
    add_cores(z)

    def more_grads(k, _):
        zz = lax.rem(z + jnp.where(k == 0, 1, jnp.where(k == 1, 3, 2)), 4)

        @pl.when(k == 2)
        def _():
            drain(cot_block(zo, 0, QD), agf_r.at[0])
            drain(cot_block(zo, QD, QD), agf_r.at[1])
            to_sibling(zo)

        drain(other_half(zz), sib_r.at[zz])
        slot_grads(zz)
        return 0

    lax.fori_loop(0, 3, more_grads, 0)

    unswap = one(
        (iota((MAIN, MAIN), 1) // 64 == (iota((MAIN, MAIN), 0) // 4) % 4)
        & ((iota((MAIN, MAIN), 1) // 4) % 16 == iota((MAIN, MAIN), 0) // 16)
        & (iota((MAIN, MAIN), 1) % 4 == iota((MAIN, MAIN), 0) % 4)
    )
    hpx[...] = sum(
        dot(unswap[:, zz * EXT : (zz + 1) * EXT], hp[zz * ROWS + MAIN : (zz + 1) * ROWS, :])
        for zz in range(NZ)
    ).astype(BF)
    send_slots(lambda p2: rows(hpx, p2 * 16, 16), p * 16, rx, ret_s.at[4], ret_r.at[4])

    drain(r1.at[0], rs_r.at[0])
    add_into(zp, 0, QD, lambda i: r1.at[0, pl.ds(mult(i * 32, 16), 32)])
    remote(out_block(zp, 0), r2_half(0, 0), rs_s.at[4], rs_r.at[4], up).start()
    drain(r1.at[1], rs_r.at[1])
    add_into(zm, QD, QD, lambda i: r1.at[1, pl.ds(mult(i * 32, 16), 32)])
    remote(out_block(zm, QD), r2_half(1, QD), rs_s.at[5], rs_r.at[5], down).start()

    for zz in range(NZ):
        drain(pa.at[0, 0:ROWS], po_s.at[zz])

    def weight_tile(j):
        src = pa.at[nc, pl.ds(0, FB), cols(lax.rem(j, 4) * XD, XD)]
        return src, local(src, wg.at[:, cols(j * XD, XD)], wg_sem.at[lax.rem(j, 4)])

    def weight_grads(j, _):
        src, copy = weight_tile(j)

        @pl.when(j >= 4)
        def _():
            copy.wait()

        src[...] = dot_tn(h[...], cot[:, cols(j * XD, XD)]).astype(BF)
        copy.start()
        return 0

    lax.fori_loop(0, 8, weight_grads, 0)

    drain(rx, ret_r.at[4])

    def tokens_grad(zz, _):
        at = pl.ds(mult(zz * MAIN, 16), MAIN)
        drain(rm.at[at], ret_r.at[zz])
        grads = dot_tn(table(zz), rm[at, :])
        late = dot_tn(extra_pick(zz, zz), rx[...])
        xh[pl.ds(mult(zz * MAIN, 16), TOK), :] = grads[0:TOK, :].astype(BF)
        xh[pl.ds(mult(zz * MAIN + TOK, 16), TOK), :] = (grads[TOK:, :] + late).astype(BF)
        return 0

    lax.fori_loop(0, NZ, tokens_grad, 0)

    drain(r2_half(0, 0), rs_r.at[4])
    drain(r2_half(0, QD), rs_r.at[2])
    add_into(z, 0, HD, lambda i: r2.at[0, pl.ds(mult(i * 32, 16), 32)])
    drain(r2_half(1, 0), rs_r.at[3])
    drain(r2_half(1, QD), rs_r.at[5])
    add_into(z, 0, HD, lambda i: r2.at[1, pl.ds(mult(i * 32, 16), 32)])
    back = (iota((MAIN, EXT), 1) // 4 == iota((MAIN, EXT), 0) // 16) & (
        iota((MAIN, EXT), 1) % 4 == iota((MAIN, EXT), 0) % 4
    )
    tail = mine_out[pl.ds(mult(z * ROWS + MAIN, 16), EXT), :]
    ex[...] = sum(
        dot(one(back & ((iota((MAIN, EXT), 0) // 4) % 4 == q)), tail[:, q * XD : (q + 1) * XD])
        for q in range(4)
    ).astype(BF)
    send_slots(
        lambda p2: mine_out.at[pl.ds(mult(z * ROWS + p2 * 16, 16), 16)],
        p * 16,
        em,
        eo_s.at[0],
        eo_r.at[0],
    )
    send_slots(lambda p2: rows(ex, p2 * 16, 16), p * 16, exr, eo_s.at[1], eo_r.at[1])

    def return_grads(piece, _):
        for dc, dz in COLUMN:
            c2, z2, dev = column(dc, dz)
            src = rows(xh, (z2 * 2 + c2) * TOK + piece * 32, 32)
            dst = hg.at[pl.ds(mult(piece * 32, 16), 32), cols(blk * FB, FB)]
            remote(src, dst, hg_s.at[0], hg_r.at[0], dev).start()
        return 0

    lax.fori_loop(0, 4, return_grads, 0)
    local(rows(xh, (z * 2 + c) * TOK, TOK), hg.at[:, cols(blk * FB, FB)], hg_r.at[0]).start()

    drain(em, eo_r.at[0])
    drain(exr, eo_r.at[1])
    kk[...] = dot_tn(table(z), em[...]).astype(BF)
    for q in range(4):
        at = slice(q * XD, (q + 1) * XD)
        kk[TOK : 2 * TOK, at] = (
            kk[TOK : 2 * TOK, at].astype(F32) + dot_tn(extra_pick(z, q), exr[...])
        ).astype(BF)
    remote(rows(kk, nc * TOK, TOK), kr, k_s.at[0], k_r.at[0], sib).start()
    picked = kk[pl.ds(mult(c * TOK, 16), TOK), :].astype(F32)
    total = jnp.sum(og[:, cols(c * HD, HD)].astype(F32) * picked, axis=1, keepdims=True)
    mixed[:, cols(c * HD, HD)] = (gate * picked).astype(BF)
    drain(kr, k_r.at[0])
    picked2 = kr[...].astype(F32)
    total += jnp.sum(og[:, cols(nc * HD, HD)].astype(F32) * picked2, axis=1, keepdims=True)
    mixed[:, cols(nc * HD, HD)] = (gate * picked2).astype(BF)
    gg[...] = jnp.sum(jnp.where(eye, total, 0.0), axis=0, keepdims=True)

    drain(hg, hg_r.at[0])
    for j in range(4):
        weight_tile(j)[1].wait()
    drain(rows(posv, 0, 56, 8), pos_s.at[0])
    drain(xh.at[pl.ds(0, 7 * TOK)], hz_s.at[0])
    drain(xh.at[pl.ds(0, 7 * TOK)], hg_s.at[0])
    drain(tsend, t_s.at[0])
    drain(gm.at[pl.ds(0, 240)], cm_s.at[0])
    drain(gx.at[pl.ds(0, 240)], cx_s.at[0])
    for n in range(5):
        drain(hp.at[pl.ds(0, 240)], hm_s.at[n])
        drain(hp.at[pl.ds(0, 240)], ret_s.at[n])
    for n in range(4):
        drain(r1.at[0], ag_s.at[n])
        drain(r2.at[0], sib_s.at[n])
    for n in range(2):
        drain(r1.at[0], agf_s.at[n])
    for n in range(6):
        drain(r1.at[0], rs_s.at[n])
    drain(em.at[pl.ds(0, 240)], eo_s.at[0])
    drain(exr.at[pl.ds(0, 240)], eo_s.at[1])
    drain(kr, k_s.at[0])


def layer(hidden_in, weights, gates, group_ids, slot_ids, out_grad):
    position = jnp.broadcast_to((group_ids * CAP + slot_ids)[None, :], (8, TOK))
    vmem = pl.BlockSpec(memory_space=pltpu.VMEM)
    anywhere = pl.BlockSpec(memory_space=pl.ANY)
    sem = pltpu.SemaphoreType.DMA

    def buf(*shape):
        return pltpu.VMEM(shape, BF)

    mixed, hidden_grad, weight_grad, gate_grad = pl.pallas_call(
        kernel,
        out_shape=(
            jax.ShapeDtypeStruct((TOK, D), BF),
            jax.ShapeDtypeStruct((TOK, FF), BF),
            jax.ShapeDtypeStruct((FB, D), BF),
            jax.ShapeDtypeStruct((1, TOK), F32),
        ),
        in_specs=[anywhere, anywhere, vmem, vmem, anywhere],
        out_specs=(vmem, anywhere, anywhere, vmem),
        scratch_shapes=[
            buf(FB, D),
            buf(NZ * ROWS, FB),
            buf(MAIN, FB),
            buf(NZ * ROWS, D),
            buf(MAIN, XD),
            buf(8 * TOK, FB),
            buf(NZ * MAIN, FB),
            buf(MAIN, FB),
            buf(2 * TOK, HD),
            buf(TOK, HD),
            buf(MAIN, HD),
            buf(MAIN, XD),
            buf(2, NZ * ROWS, HD),
            buf(NZ * ROWS, HD),
            buf(2, ROWS, QD),
            buf(2, ROWS, HD),
            buf(MAIN, XD),
            buf(MAIN, HD),
            buf(MAIN, XD),
            buf(NZ * ROWS, FB),
            buf(MAIN, FB),
            buf(NZ * MAIN, FB),
            buf(MAIN, FB),
            buf(2 * TOK, HD),
            buf(TOK, HD),
            buf(TOK, D),
            buf(NZ * MAIN, 2 * TOK),
            buf(NZ * MAIN, TOK),
            pltpu.VMEM((8 * 8, TOK), jnp.int32),
            sem((1,)), sem((1,)),
            sem((1,)), sem((1,)),
            sem((1,)), sem((1,)),
            sem((1,)), sem((1,)),
            sem((1,)), sem((1,)),
            sem((1,)), sem((1,)),
            sem((5,)), sem((5,)),
            sem((4,)), sem((4,)),
            sem((2,)), sem((2,)),
            sem((4,)), sem((4,)),
            sem((4,)), sem((4,)),
            sem((6,)), sem((6,)),
            sem((5,)), sem((5,)),
            sem((2,)), sem((2,)),
            sem((1,)), sem((1,)),
            sem((1,)), sem((1,)),
            sem((4,)),
        ],
        compiler_params=pltpu.CompilerParams(
            collective_id=0, has_side_effects=True, vmem_limit_bytes=64 * 1024 * 1024 - 65536
        ),
        cost_estimate=pl.CostEstimate(
            flops=6 * NZ * ROWS * FB * D, bytes_accessed=20_000_000, transcendentals=0
        ),
        name="experts",
    )(hidden_in, weights, gates.reshape(1, TOK), position, out_grad)
    return mixed, hidden_grad, weight_grad, gate_grad.reshape(TOK)


def solution(mesh):
    wide, flat = P(("grp", "exp"), None), P(("grp", "exp"))
    return jax.shard_map(
        layer,
        mesh=mesh,
        in_specs=(wide, wide, flat, flat, flat, wide),
        out_specs=(wide, wide, wide, flat),
        check_vma=False,
    )
```

```python
import functools

import jax
import jax.numpy as jnp
from jax import lax
from jax.experimental import pallas as pl
from jax.experimental.pallas import tpu as pltpu
from jax.sharding import PartitionSpec as P

MESH = pl.DeviceIdType.MESH
BF = jnp.bfloat16
F32 = jnp.float32
TOK, CAP = 128, 10
D, FF, FB = 4096, 7168, 896
HD, QD, XD = D // 2, D // 4, D // 8
NP, NZ = 16, 4
MAIN, EXT, ROWS = 256, 64, 320


def hops(k):
    return min(k, 4 - k)


PLANE = sorted(
    [(i, j) for i in range(4) for j in range(4) if i + j], key=lambda o: -(hops(o[0]) + hops(o[1]))
)
COLUMN = [(0, 2), (1, 2), (0, 1), (0, 3), (1, 1), (1, 3), (1, 0)]


def dot(a, b, dims=((1,), (0,))):
    return lax.dot_general(a, b, (dims, ((), ())), preferred_element_type=F32)


def dot_tn(a, b):
    return dot(a, b, ((0,), (0,)))


def dot_nt(a, b):
    return dot(a, b, ((1,), (1,)))


def one(cond):
    return jnp.where(cond, 1.0, 0.0).astype(F32).astype(BF)


def iota(shape, dim):
    return lax.broadcasted_iota(jnp.int32, shape, dim)


def mult(value, of):
    return pl.multiple_of(value, of)


def kernel(
    hid, w_hbm, gates, group_ids, slot_ids, og_hbm,
    picked, hg, wg,
    wv, h, hxr, cot, cxp, xh, sm, sx, tok, tsend, gm, gx, pa, prcv, r1, r2, ex, em, exr, hp, hpx, rm, rx, kk, og,
    mt, xb, posv,
    pos_s, pos_r, hz_s, hz_r, w_sem, og_sem, st_sem, t_s, t_r, cm_s, cm_r, cx_s, cx_r, hm_s, hm_r,
    ag_s, ag_r, agf_s, agf_r, sib_s, sib_r, po_s, po_r, rs_s, rs_r, ret_s, ret_r, eo_s, eo_r, k_s, k_r, hg_s, hg_r, wg_sem,
):
    g = lax.axis_index("grp")
    z = lax.axis_index("exp")
    c = lax.rem(g, 2)
    p = lax.div(g, 2)
    x = lax.div(p, 4)
    y = lax.rem(p, 4)
    nc = 1 - c
    zp = lax.rem(z + 1, 4)
    zm = lax.rem(z + 3, 4)
    zo = lax.rem(z + 2, 4)
    sib = (p * 2 + nc, z)
    up = (g, zp)
    down = (g, zm)
    blk = c * 4 + z

    def plane(i, j):
        p2 = lax.rem(x + i, 4) * 4 + lax.rem(y + j, 4)
        return p2, (p2 * 2 + c, z)

    def column(dc, dz):
        c2 = lax.rem(c + dc, 2)
        z2 = lax.rem(z + dz, 4)
        return c2, z2, (p * 2 + c2, z2)

    def remote(src, dst, ss, rs, dev):
        return pltpu.make_async_remote_copy(
            src_ref=src, dst_ref=dst, send_sem=ss, recv_sem=rs, device_id=dev, device_id_type=MESH
        )

    def local(src, dst, sem):
        return pltpu.make_async_copy(src, dst, sem)

    def drain(ref, sem):
        pltpu.make_async_copy(ref, ref, sem).wait()

    def rows(ref, start, size, of=16):
        return ref.at[pl.ds(mult(start, of), size)]

    def cols(start, size):
        return pl.ds(mult(start, 128), size)

    barrier = pltpu.get_barrier_semaphore()
    for dc, dz in COLUMN:
        pl.semaphore_signal(barrier, inc=1, device_id=column(dc, dz)[2], device_id_type=MESH)
    for i, j in PLANE:
        pl.semaphore_signal(barrier, inc=1, device_id=plane(i, j)[1], device_id_type=MESH)

    local(og_hbm, og, og_sem.at[0]).start()
    for k in range(8):
        local(hid.at[:, pl.ds(k * FB, FB)], hp.at[pl.ds(k * TOK, TOK)], st_sem.at[0]).start()
    local(w_hbm, wv, w_sem.at[0]).start()
    position = group_ids[...] * CAP + slot_ids[...]
    posv[pl.ds(mult((z * 2 + c) * 8, 8), 8), :] = jnp.broadcast_to(position, (8, TOK))
    eye = iota((TOK, TOK), 0) == iota((TOK, TOK), 1)
    gate = jnp.sum(jnp.where(eye, gates[...], 0.0), axis=1, keepdims=True)
    drain(og, og_sem.at[0])
    tsend[...] = (gate * og[:, cols(nc * HD, HD)].astype(F32)).astype(BF)
    drain(hp.at[pl.ds(0, 8 * TOK)], st_sem.at[0])
    pl.semaphore_wait(barrier, len(COLUMN) + len(PLANE))

    remote(tsend, rows(tok, c * TOK, TOK), t_s.at[0], t_r.at[0], sib).start()
    mine = rows(posv, (z * 2 + c) * 8, 8, 8)
    for dc, dz in COLUMN:
        remote(mine, mine, pos_s.at[0], pos_r.at[0], column(dc, dz)[2]).start()

    def send_hidden(piece, _):
        for dc, dz in COLUMN:
            c2, z2, dev = column(dc, dz)
            src = rows(hp, (c2 * 4 + z2) * TOK + piece * 32, 32)
            dst = rows(xh, (z * 2 + c) * TOK + piece * 32, 32)
            remote(src, dst, hz_s.at[0], hz_r.at[0], dev).start()
        return 0

    lax.fori_loop(0, 4, send_hidden, 0)
    local(rows(hp, blk * TOK, TOK), rows(xh, (z * 2 + c) * TOK, TOK), hz_r.at[0]).start()
    tok[pl.ds(mult(c * TOK, 16), TOK), :] = (gate * og[:, cols(c * HD, HD)].astype(F32)).astype(BF)

    drain(rows(posv, 0, 56, 8), pos_r.at[0])

    def tables(zz, _):
        group = iota((MAIN, TOK), 0) // 16
        slot = iota((MAIN, TOK), 0) % 16
        both = posv[pl.ds(mult(zz * 16, 16), 16), :]
        first, second = both[0:1, :], both[8:9, :]
        at = pl.ds(mult(zz * MAIN, 16), MAIN)
        mt[at, 0:TOK] = one((slot < CAP) & (group * CAP + slot == first))
        mt[at, TOK : 2 * TOK] = one((slot >= CAP) & (group * CAP + slot - CAP == second))
        xb[at, :] = one(group * CAP + slot % 4 + 6 == second)
        return 0

    lax.fori_loop(0, NZ, tables, 0)
    part = (iota((MAIN, TOK), 0) // 4) % 4

    def extra_pick(zz, q):
        base = xb[pl.ds(mult(zz * MAIN, 16), MAIN), :]
        return jnp.where(part == q, base.astype(F32), 0.0).astype(BF)

    def table(zz):
        return mt[pl.ds(mult(zz * MAIN, 16), MAIN), :]

    def half(ref, start, size, n):
        return ref.at[pl.ds(mult(start, 16), size), pl.ds(n * QD, QD)]

    def cot_half(start, size, n):
        return cot.at[pl.ds(mult(start, 16), size), cols(c * HD + n * QD, QD)]

    def send_slots(src, dst, ss, rs):
        for i, j in PLANE:
            p2, dev = plane(i, j)
            remote(src(p2), dst, ss, rs, dev).start()
        local(src(p), dst, rs).start()

    drain(tsend, t_r.at[0])
    gx[...] = sum(
        dot(extra_pick(z, q), tok[TOK : 2 * TOK, q * XD : (q + 1) * XD]) for q in range(4)
    ).astype(BF)
    send_slots(lambda p2: rows(gx, p2 * 16, 16), rows(cxp, p * 16, 16), cx_s.at[0], cx_r.at[0])
    for n in range(2):
        gm[:, n * QD : (n + 1) * QD] = dot(table(z), tok[:, n * QD : (n + 1) * QD]).astype(BF)
        send_slots(
            lambda p2: half(gm, p2 * 16, 16, n), cot_half(z * ROWS + p * 16, 16, n), cm_s.at[n], cm_r.at[n]
        )

    def cot_block(zz, start, size):
        return cot.at[pl.ds(mult(zz * ROWS, 16), ROWS), cols(c * HD + start, size)]

    def to_sibling(zz):
        ref = cot_block(zz, 0, HD)
        remote(ref, ref, sib_s.at[zz], sib_r.at[zz], sib).start()

    drain(cxp, cx_r.at[0])
    place = (iota((EXT, MAIN), 0) // 4 == iota((EXT, MAIN), 1) // 16) & (
        iota((EXT, MAIN), 0) % 4 == iota((EXT, MAIN), 1) % 4
    )
    for q in range(4):
        unpack = one(place & ((iota((EXT, MAIN), 1) // 4) % 4 == q))
        cot[pl.ds(mult(z * ROWS + MAIN, 16), EXT), cols(c * HD + q * XD, XD)] = dot(
            unpack, cxp[...]
        ).astype(BF)
    for n in range(2):
        drain(cot_half(z * ROWS, MAIN, n), cm_r.at[n])
        ref = cot_block(z, n * QD, QD)
        remote(ref, ref, ag_s.at[2 * n], ag_r.at[2 * n], up).start()
        remote(ref, ref, ag_s.at[2 * n + 1], ag_r.at[2 * n + 1], down).start()
    to_sibling(z)

    drain(xh, hz_r.at[0])
    sx[...] = sum(
        dot(extra_pick(zz, zz), xh[(2 * zz + 1) * TOK : (2 * zz + 2) * TOK, :]) for zz in range(NZ)
    ).astype(BF)

    send_slots(lambda p2: rows(sx, p2 * 16, 16), rows(hxr, p * 16, 16), hm_s.at[4], hm_r.at[4])

    def order(k):
        return lax.rem(z + jnp.where(k == 2, 3, jnp.where(k == 3, 0, 2 - k)), 4)

    def pick_hidden(k, _):
        zz = order(k)
        at = pl.ds(mult(zz * MAIN, 16), MAIN)
        sm[at, :] = dot(table(zz), xh[at, :]).astype(BF)
        send_slots(
            lambda p2: rows(sm, zz * MAIN + p2 * 16, 16),
            rows(h, zz * ROWS + p * 16, 16),
            hm_s.at[zz],
            hm_r.at[zz],
        )
        return 0

    lax.fori_loop(0, NZ, pick_hidden, 0)

    drain(wv, w_sem.at[0])

    drain(hp.at[pl.ds(0, 7 * TOK)], hz_s.at[0])

    def slot_grads(zz):
        at = pl.ds(mult(zz * ROWS, 16), ROWS)
        hp[at, :] = dot_nt(cot[at, :], wv[...]).astype(BF)
        send_slots(
            lambda p2: rows(hp, zz * ROWS + p2 * 16, 16),
            rows(rm, zz * MAIN + p * 16, 16),
            ret_s.at[zz],
            ret_r.at[zz],
        )

    def other_half(zz):
        return cot.at[pl.ds(mult(zz * ROWS, 16), ROWS), cols(nc * HD, HD)]

    drain(other_half(z), sib_r.at[z])
    slot_grads(z)

    mine_out = pa.at[c]
    drain(hxr, hm_r.at[4])
    swap = one(
        (iota((MAIN, MAIN), 0) // 64 == (iota((MAIN, MAIN), 1) // 4) % 4)
        & ((iota((MAIN, MAIN), 0) // 4) % 16 == iota((MAIN, MAIN), 1) // 16)
        & (iota((MAIN, MAIN), 0) % 4 == iota((MAIN, MAIN), 1) % 4)
    )
    moved = dot(swap, hxr[...]).astype(BF)
    for zz in range(NZ):
        h[zz * ROWS + MAIN : (zz + 1) * ROWS, :] = moved[zz * EXT : (zz + 1) * EXT, :]

    def add_into(zz, start, size, ref):
        def step(i, _):
            at = pl.ds(mult(zz * ROWS + i * 32, 16), 32)
            where = cols(start, size)
            mine_out[at, where] = (
                mine_out[at, where].astype(F32) + ref(i)[...].astype(F32)
            ).astype(BF)
            return 0

        lax.fori_loop(0, ROWS // 32, step, 0)

    def add_cores(zz):
        drain(prcv.at[pl.ds(mult(zz * ROWS, 16), ROWS)], po_r.at[zz])
        add_into(zz, 0, HD, lambda i: prcv.at[pl.ds(mult(zz * ROWS + i * 32, 16), 32)])

    def out_block(zz, start):
        return mine_out.at[pl.ds(mult(zz * ROWS, 16), ROWS), pl.ds(start, QD)]

    def r2_half(n, start):
        return r2.at[n, :, pl.ds(start, QD)]

    def partials(k, _):
        zz = order(k)
        at = pl.ds(mult(zz * ROWS, 16), ROWS)

        @pl.when(k == 0)
        def _():
            drain(cot_block(zm, 0, QD), ag_r.at[0])
            ref = cot_block(zm, 0, QD)
            remote(ref, ref, agf_s.at[0], agf_r.at[0], up).start()
            drain(cot_block(zp, QD, QD), ag_r.at[3])
            ref2 = cot_block(zp, QD, QD)
            remote(ref2, ref2, agf_s.at[1], agf_r.at[1], down).start()

        drain(h.at[pl.ds(mult(zz * ROWS, 16), MAIN)], hm_r.at[zz])
        rows_in = h[at, :]

        def product(half):
            def tile(j, _):
                pa[half, at, cols(j * QD, QD)] = dot(
                    rows_in, wv[:, cols(half * HD + j * QD, QD)]
                ).astype(BF)
                return 0

            lax.fori_loop(0, 2, tile, 0)

        product(nc)
        remote(
            pa.at[nc, at], prcv.at[at], po_s.at[zz], po_r.at[zz], sib
        ).start()
        product(c)

        @pl.when(k == 1)
        def _():
            add_cores(zo)
            remote(out_block(zo, 0), r1.at[0], rs_s.at[0], rs_r.at[0], up).start()
            remote(out_block(zo, QD), r1.at[1], rs_s.at[1], rs_r.at[1], down).start()

        @pl.when(k == 2)
        def _():
            add_cores(zp)
            remote(out_block(zp, QD), r2_half(0, QD), rs_s.at[2], rs_r.at[2], up).start()
            drain(cot_block(zm, QD, QD), ag_r.at[2])
            to_sibling(zm)
            drain(cot_block(zp, 0, QD), ag_r.at[1])
            to_sibling(zp)

        @pl.when(k == 3)
        def _():
            add_cores(zm)
            remote(out_block(zm, 0), r2_half(1, 0), rs_s.at[3], rs_r.at[3], down).start()

        return 0

    lax.fori_loop(0, NZ, partials, 0)
    add_cores(z)

    def more_grads(k, _):
        zz = lax.rem(z + jnp.where(k == 0, 1, jnp.where(k == 1, 3, 2)), 4)

        @pl.when(k == 2)
        def _():
            drain(cot_block(zo, 0, QD), agf_r.at[0])
            drain(cot_block(zo, QD, QD), agf_r.at[1])
            to_sibling(zo)

        drain(other_half(zz), sib_r.at[zz])
        slot_grads(zz)
        return 0

    lax.fori_loop(0, 3, more_grads, 0)

    unswap = one(
        (iota((MAIN, MAIN), 1) // 64 == (iota((MAIN, MAIN), 0) // 4) % 4)
        & ((iota((MAIN, MAIN), 1) // 4) % 16 == iota((MAIN, MAIN), 0) // 16)
        & (iota((MAIN, MAIN), 1) % 4 == iota((MAIN, MAIN), 0) % 4)
    )
    hpx[...] = sum(
        dot(unswap[:, zz * EXT : (zz + 1) * EXT], hp[zz * ROWS + MAIN : (zz + 1) * ROWS, :])
        for zz in range(NZ)
    ).astype(BF)
    send_slots(lambda p2: rows(hpx, p2 * 16, 16), rows(rx, p * 16, 16), ret_s.at[4], ret_r.at[4])

    drain(r1.at[0], rs_r.at[0])
    add_into(zp, 0, QD, lambda i: r1.at[0, pl.ds(mult(i * 32, 16), 32)])
    remote(out_block(zp, 0), r2_half(0, 0), rs_s.at[4], rs_r.at[4], up).start()
    drain(r1.at[1], rs_r.at[1])
    add_into(zm, QD, QD, lambda i: r1.at[1, pl.ds(mult(i * 32, 16), 32)])
    remote(out_block(zm, QD), r2_half(1, QD), rs_s.at[5], rs_r.at[5], down).start()

    for zz in range(NZ):
        drain(pa.at[0, 0:ROWS], po_s.at[zz])

    def weight_tile(j):
        src = pa.at[nc, pl.ds(0, FB), cols(lax.rem(j, 4) * XD, XD)]
        return src, local(src, wg.at[:, cols(j * XD, XD)], wg_sem.at[lax.rem(j, 4)])

    def weight_grads(j, _):
        src, copy = weight_tile(j)

        @pl.when(j >= 4)
        def _():
            copy.wait()

        src[...] = dot_tn(h[...], cot[:, cols(j * XD, XD)]).astype(BF)
        copy.start()
        return 0

    lax.fori_loop(0, 8, weight_grads, 0)

    drain(rx, ret_r.at[4])

    def tokens_grad(zz, _):
        at = pl.ds(mult(zz * MAIN, 16), MAIN)
        drain(rm.at[at], ret_r.at[zz])
        grads = dot_tn(table(zz), rm[at, :])
        late = dot_tn(extra_pick(zz, zz), rx[...])
        xh[pl.ds(mult(zz * MAIN, 16), TOK), :] = grads[0:TOK, :].astype(BF)
        xh[pl.ds(mult(zz * MAIN + TOK, 16), TOK), :] = (grads[TOK:, :] + late).astype(BF)
        return 0

    lax.fori_loop(0, NZ, tokens_grad, 0)

    drain(r2_half(0, 0), rs_r.at[4])
    drain(r2_half(0, QD), rs_r.at[2])
    drain(r2_half(1, 0), rs_r.at[3])
    drain(r2_half(1, QD), rs_r.at[5])

    def last_sum(first, count, start, size):
        def step(i, _):
            from_row = first + i * 32
            at = pl.ds(mult(z * ROWS + from_row, 16), 32)
            there = pl.ds(mult(from_row, 16), 32)
            where = pl.ds(start, size)
            mine_out[at, where] = (
                mine_out[at, where].astype(F32)
                + r2[0, there, where].astype(F32)
                + r2[1, there, where].astype(F32)
            ).astype(BF)
            return 0

        lax.fori_loop(0, count // 32, step, 0)

    last_sum(MAIN, EXT, 0, HD)
    back = (iota((MAIN, EXT), 1) // 4 == iota((MAIN, EXT), 0) // 16) & (
        iota((MAIN, EXT), 1) % 4 == iota((MAIN, EXT), 0) % 4
    )
    tail = mine_out[pl.ds(mult(z * ROWS + MAIN, 16), EXT), :]
    ex[...] = sum(
        dot(one(back & ((iota((MAIN, EXT), 0) // 4) % 4 == q)), tail[:, q * XD : (q + 1) * XD])
        for q in range(4)
    ).astype(BF)
    send_slots(lambda p2: rows(ex, p2 * 16, 16), rows(exr, p * 16, 16), eo_s.at[2], eo_r.at[2])
    for n in range(2):
        last_sum(0, MAIN, n * QD, QD)
        send_slots(
            lambda p2: half(mine_out, z * ROWS + p2 * 16, 16, n),
            half(em, p * 16, 16, n),
            eo_s.at[n],
            eo_r.at[n],
        )

    def return_grads(piece, _):
        for dc, dz in COLUMN:
            c2, z2, dev = column(dc, dz)
            src = rows(xh, (z2 * 2 + c2) * TOK + piece * 32, 32)
            dst = hg.at[pl.ds(mult(piece * 32, 16), 32), cols(blk * FB, FB)]
            remote(src, dst, hg_s.at[0], hg_r.at[0], dev).start()
        return 0

    lax.fori_loop(0, 4, return_grads, 0)
    local(rows(xh, (z * 2 + c) * TOK, TOK), hg.at[:, cols(blk * FB, FB)], hg_r.at[0]).start()

    drain(exr, eo_r.at[2])
    for n in range(2):
        drain(half(em, 0, MAIN, n), eo_r.at[n])
        rows_out = dot_tn(table(z), em[:, n * QD : (n + 1) * QD])
        late = jnp.concatenate([dot_tn(extra_pick(z, 2 * n + q), exr[...]) for q in range(2)], axis=1)
        kk[0:TOK, n * QD : (n + 1) * QD] = rows_out[0:TOK, :].astype(BF)
        kk[TOK : 2 * TOK, n * QD : (n + 1) * QD] = (rows_out[TOK:, :] + late).astype(BF)
        there = picked.at[:, cols(c * HD + n * QD, QD)]
        remote(half(kk, nc * TOK, TOK, n), there, k_s.at[n], k_r.at[n], sib).start()
        local(half(kk, c * TOK, TOK, n), there, k_s.at[2 + n]).start()

    for n in range(2):
        drain(picked.at[:, cols(nc * HD + n * QD, QD)], k_r.at[n])
        drain(half(kk, 0, TOK, n), k_s.at[n])
        drain(half(kk, 0, TOK, n), k_s.at[2 + n])
    drain(hg, hg_r.at[0])
    for j in range(4):
        weight_tile(j)[1].wait()
    drain(rows(posv, 0, 56, 8), pos_s.at[0])
    drain(xh.at[pl.ds(0, 7 * TOK)], hg_s.at[0])
    drain(tsend, t_s.at[0])
    for n in range(2):
        drain(half(gm, 0, 240, n), cm_s.at[n])
        drain(half(em, 0, 240, n), eo_s.at[n])
    drain(gx.at[pl.ds(0, 240)], cx_s.at[0])
    for n in range(5):
        drain(hp.at[pl.ds(0, 240)], hm_s.at[n])
        drain(hp.at[pl.ds(0, 240)], ret_s.at[n])
    for n in range(4):
        drain(r1.at[0], ag_s.at[n])
        drain(r2.at[0], sib_s.at[n])
    for n in range(2):
        drain(r1.at[0], agf_s.at[n])
    for n in range(6):
        drain(r1.at[0], rs_s.at[n])
    drain(exr.at[pl.ds(0, 240)], eo_s.at[2])


PIECES = 8


def finish(
    picked_hbm, gates, og_hbm, hg_in, wg_in, mixed, hg, wg, gg, picked, og, out, hbuf, wbuf, in_sem, out_sem
):
    copies = []
    for k in range(PIECES):
        at = pl.ds(k * (FB // PIECES), FB // PIECES)
        copies.append((wg_in.at[at], wbuf.at[at], wg.at[at]))
    for k in range(2):
        at = pl.ds(k * (TOK // 2), TOK // 2)
        copies.append((hg_in.at[at], hbuf.at[at], hg.at[at]))
    loads = [pltpu.make_async_copy(a, b, in_sem.at[k]) for k, (a, b, _) in enumerate(copies)]
    stores = [pltpu.make_async_copy(b, a, out_sem.at[k]) for k, (_, b, a) in enumerate(copies)]
    rows_in = [
        pltpu.make_async_copy(picked_hbm, picked, in_sem.at[PIECES + 2]),
        pltpu.make_async_copy(og_hbm, og, in_sem.at[PIECES + 3]),
    ]
    for copy in rows_in + loads:
        copy.start()
    eye = iota((TOK, TOK), 0) == iota((TOK, TOK), 1)
    gate = jnp.sum(jnp.where(eye, gates[...], 0.0), axis=1, keepdims=True)
    for copy in rows_in:
        copy.wait()
    rows = picked[...].astype(F32)
    out[...] = (gate * rows).astype(BF)
    store = pltpu.make_async_copy(out, mixed, out_sem.at[PIECES + 2])
    store.start()
    for load, copy in zip(loads[:4], stores):
        load.wait()
        copy.start()
    total = jnp.sum(og[...].astype(F32) * rows, axis=1, keepdims=True)
    gg[...] = jnp.sum(jnp.where(eye, total, 0.0), axis=0, keepdims=True)
    for load, copy in zip(loads[4:], stores[4:]):
        load.wait()
        copy.start()
    for copy in stores + [store]:
        copy.wait()


def layer(hidden_in, weights, gates, group_ids, slot_ids, out_grad):
    vmem = pl.BlockSpec(memory_space=pltpu.VMEM)
    anywhere = pl.BlockSpec(memory_space=pl.ANY)
    sem = pltpu.SemaphoreType.DMA

    def buf(*shape):
        return pltpu.VMEM(shape, BF)

    gate_row = gates.reshape(1, TOK)
    picked, hidden_grad, weight_grad = pl.pallas_call(
        kernel,
        out_shape=(
            jax.ShapeDtypeStruct((TOK, D), BF),
            jax.ShapeDtypeStruct((TOK, FF), BF),
            jax.ShapeDtypeStruct((FB, D), BF),
        ),
        in_specs=[anywhere, anywhere, vmem, vmem, vmem, anywhere],
        out_specs=(anywhere, anywhere, anywhere),
        scratch_shapes=[
            buf(FB, D),
            buf(NZ * ROWS, FB),
            buf(MAIN, FB),
            buf(NZ * ROWS, D),
            buf(MAIN, XD),
            buf(8 * TOK, FB),
            buf(NZ * MAIN, FB),
            buf(MAIN, FB),
            buf(2 * TOK, HD),
            buf(TOK, HD),
            buf(MAIN, HD),
            buf(MAIN, XD),
            buf(2, NZ * ROWS, HD),
            buf(NZ * ROWS, HD),
            buf(2, ROWS, QD),
            buf(2, ROWS, HD),
            buf(MAIN, XD),
            buf(MAIN, HD),
            buf(MAIN, XD),
            buf(NZ * ROWS, FB),
            buf(MAIN, FB),
            buf(NZ * MAIN, FB),
            buf(MAIN, FB),
            buf(2 * TOK, HD),
            buf(TOK, D),
            buf(NZ * MAIN, 2 * TOK),
            buf(NZ * MAIN, TOK),
            pltpu.VMEM((8 * 8, TOK), jnp.int32),
            sem((1,)), sem((1,)),
            sem((1,)), sem((1,)),
            sem((1,)), sem((1,)), sem((1,)),
            sem((1,)), sem((1,)),
            sem((2,)), sem((2,)),
            sem((1,)), sem((1,)),
            sem((5,)), sem((5,)),
            sem((4,)), sem((4,)),
            sem((2,)), sem((2,)),
            sem((4,)), sem((4,)),
            sem((4,)), sem((4,)),
            sem((6,)), sem((6,)),
            sem((5,)), sem((5,)),
            sem((3,)), sem((3,)),
            sem((4,)), sem((2,)),
            sem((1,)), sem((1,)),
            sem((4,)),
        ],
        compiler_params=pltpu.CompilerParams(
            collective_id=0, has_side_effects=True, vmem_limit_bytes=64 * 1024 * 1024 - 65536
        ),
        cost_estimate=pl.CostEstimate(
            flops=6 * NZ * ROWS * FB * D, bytes_accessed=20_000_000, transcendentals=0
        ),
        name="experts",
    )(hidden_in, weights, gate_row, group_ids.reshape(1, TOK), slot_ids.reshape(1, TOK), out_grad)

    mixed, hidden_grad, weight_grad, gate_grad = pl.pallas_call(
        finish,
        out_shape=(
            jax.ShapeDtypeStruct((TOK, D), BF),
            jax.ShapeDtypeStruct((TOK, FF), BF),
            jax.ShapeDtypeStruct((FB, D), BF),
            jax.ShapeDtypeStruct((1, TOK), F32),
        ),
        in_specs=[anywhere, vmem, anywhere, anywhere, anywhere],
        out_specs=(anywhere, anywhere, anywhere, vmem),
        scratch_shapes=[
            buf(TOK, D), buf(TOK, D), buf(TOK, D), buf(TOK, FF), buf(FB, D),
            sem((PIECES + 4,)), sem((PIECES + 3,)),
        ],
        compiler_params=pltpu.CompilerParams(vmem_limit_bytes=64 * 1024 * 1024 - 65536),
        name="finish",
    )(picked, gate_row, out_grad, hidden_grad, weight_grad)
    return mixed, hidden_grad, weight_grad, gate_grad.reshape(TOK)


def solution(mesh):
    wide, flat = P(("grp", "exp"), None), P(("grp", "exp"))
    return jax.shard_map(
        layer,
        mesh=mesh,
        in_specs=(wide, wide, flat, flat, flat, wide),
        out_specs=(wide, wide, wide, flat),
        check_vma=False,
    )
```

```python
import functools

import jax
import jax.numpy as jnp
from jax import lax
from jax.experimental import pallas as pl
from jax.experimental.pallas import tpu as pltpu
from jax.sharding import PartitionSpec as P

MESH = pl.DeviceIdType.MESH
BF = jnp.bfloat16
F32 = jnp.float32
TOK, CAP = 128, 10
D, FF, FB = 4096, 7168, 896
HD, QD, XD = D // 2, D // 4, D // 8
NP, NZ = 16, 4
MAIN, EXT, ROWS = 256, 64, 320


def hops(k):
    return min(k, 4 - k)


PLANE = sorted(
    [(i, j) for i in range(4) for j in range(4) if i + j], key=lambda o: -(hops(o[0]) + hops(o[1]))
)
COLUMN = [(0, 2), (1, 2), (0, 1), (0, 3), (1, 1), (1, 3), (1, 0)]


def dot(a, b, dims=((1,), (0,))):
    return lax.dot_general(a, b, (dims, ((), ())), preferred_element_type=F32)


def dot_tn(a, b):
    return dot(a, b, ((0,), (0,)))


def dot_nt(a, b):
    return dot(a, b, ((1,), (1,)))


def one(cond):
    return jnp.where(cond, 1.0, 0.0).astype(F32).astype(BF)


def iota(shape, dim):
    return lax.broadcasted_iota(jnp.int32, shape, dim)


def mult(value, of):
    return pl.multiple_of(value, of)


def kernel(
    hid, w_hbm, gates, group_ids, slot_ids, og_hbm,
    picked, hg, wg,
    wv, h, hxr, cot, cxp, xh, sm, sx, tok, tsend, gm, gx, pa, prcv, r1, r2, em, exr, hp, rm, rx, og,
    mt, xb, posv,
    pos_s, pos_r, hz_s, hz_r, w_sem, og_sem, st_sem, t_s, t_r, cm_s, cm_r, cx_s, cx_r, hm_s, hm_r,
    ag_s, ag_r, agf_s, agf_r, sib_s, sib_r, po_s, po_r, rs_s, rs_r, ret_s, ret_r, eo_s, eo_r, k_s, k_r, hg_s, hg_r,
):
    g = lax.axis_index("grp")
    z = lax.axis_index("exp")
    c = lax.rem(g, 2)
    p = lax.div(g, 2)
    x = lax.div(p, 4)
    y = lax.rem(p, 4)
    nc = 1 - c
    zp = lax.rem(z + 1, 4)
    zm = lax.rem(z + 3, 4)
    zo = lax.rem(z + 2, 4)
    sib = (p * 2 + nc, z)
    up = (g, zp)
    down = (g, zm)
    blk = c * 4 + z
    kk, hpx, ex = tok, sx, gx

    def plane(i, j):
        p2 = lax.rem(x + i, 4) * 4 + lax.rem(y + j, 4)
        return p2, (p2 * 2 + c, z)

    def column(dc, dz):
        c2 = lax.rem(c + dc, 2)
        z2 = lax.rem(z + dz, 4)
        return c2, z2, (p * 2 + c2, z2)

    def remote(src, dst, ss, rs, dev):
        return pltpu.make_async_remote_copy(
            src_ref=src, dst_ref=dst, send_sem=ss, recv_sem=rs, device_id=dev, device_id_type=MESH
        )

    def local(src, dst, sem):
        return pltpu.make_async_copy(src, dst, sem)

    def drain(ref, sem):
        pltpu.make_async_copy(ref, ref, sem).wait()

    def rows(ref, start, size, of=16):
        return ref.at[pl.ds(mult(start, of), size)]

    def cols(start, size):
        return pl.ds(mult(start, 128), size)

    barrier = pltpu.get_barrier_semaphore()
    for dc, dz in COLUMN:
        pl.semaphore_signal(barrier, inc=1, device_id=column(dc, dz)[2], device_id_type=MESH)
    for i, j in PLANE:
        pl.semaphore_signal(barrier, inc=1, device_id=plane(i, j)[1], device_id_type=MESH)

    local(og_hbm, og, og_sem.at[0]).start()
    for k in range(8):
        local(hid.at[:, pl.ds(k * FB, FB)], hp.at[pl.ds(k * TOK, TOK)], st_sem.at[0]).start()
    local(w_hbm, wv, w_sem.at[0]).start()
    position = group_ids[...] * CAP + slot_ids[...]
    posv[pl.ds(mult((z * 2 + c) * 8, 8), 8), :] = jnp.broadcast_to(position, (8, TOK))
    eye = iota((TOK, TOK), 0) == iota((TOK, TOK), 1)
    gate = jnp.sum(jnp.where(eye, gates[...], 0.0), axis=1, keepdims=True)
    drain(og, og_sem.at[0])
    tsend[...] = (gate * og[:, cols(nc * HD, HD)].astype(F32)).astype(BF)
    drain(hp.at[pl.ds(0, 8 * TOK)], st_sem.at[0])
    pl.semaphore_wait(barrier, len(COLUMN) + len(PLANE))

    remote(tsend, rows(tok, c * TOK, TOK), t_s.at[0], t_r.at[0], sib).start()
    mine = rows(posv, (z * 2 + c) * 8, 8, 8)
    for dc, dz in COLUMN:
        remote(mine, mine, pos_s.at[0], pos_r.at[0], column(dc, dz)[2]).start()

    def send_hidden(piece, _):
        for dc, dz in COLUMN:
            c2, z2, dev = column(dc, dz)
            src = rows(hp, (c2 * 4 + z2) * TOK + piece * 32, 32)
            dst = rows(xh, (z * 2 + c) * TOK + piece * 32, 32)
            remote(src, dst, hz_s.at[0], hz_r.at[0], dev).start()
        return 0

    lax.fori_loop(0, 4, send_hidden, 0)
    local(rows(hp, blk * TOK, TOK), rows(xh, (z * 2 + c) * TOK, TOK), hz_r.at[0]).start()
    tok[pl.ds(mult(c * TOK, 16), TOK), :] = (gate * og[:, cols(c * HD, HD)].astype(F32)).astype(BF)

    drain(rows(posv, 0, 56, 8), pos_r.at[0])

    def tables(zz, _):
        group = iota((MAIN, TOK), 0) // 16
        slot = iota((MAIN, TOK), 0) % 16
        both = posv[pl.ds(mult(zz * 16, 16), 16), :]
        first, second = both[0:1, :], both[8:9, :]
        at = pl.ds(mult(zz * MAIN, 16), MAIN)
        mt[at, 0:TOK] = one((slot < CAP) & (group * CAP + slot == first))
        mt[at, TOK : 2 * TOK] = one((slot >= CAP) & (group * CAP + slot - CAP == second))
        xb[at, :] = one(group * CAP + slot % 4 + 6 == second)
        return 0

    lax.fori_loop(0, NZ, tables, 0)
    part = (iota((MAIN, TOK), 0) // 4) % 4

    def extra_pick(zz, q):
        base = xb[pl.ds(mult(zz * MAIN, 16), MAIN), :]
        return jnp.where(part == q, base.astype(F32), 0.0).astype(BF)

    def table(zz):
        return mt[pl.ds(mult(zz * MAIN, 16), MAIN), :]

    def half(ref, start, size, n):
        return ref.at[pl.ds(mult(start, 16), size), pl.ds(n * QD, QD)]

    def cot_half(start, size, n):
        return cot.at[pl.ds(mult(start, 16), size), cols(c * HD + n * QD, QD)]

    def send_slots(src, dst, ss, rs):
        for i, j in PLANE:
            p2, dev = plane(i, j)
            remote(src(p2), dst, ss, rs, dev).start()
        local(src(p), dst, rs).start()

    drain(tsend, t_r.at[0])
    gx[...] = sum(
        dot(extra_pick(z, q), tok[TOK : 2 * TOK, q * XD : (q + 1) * XD]) for q in range(4)
    ).astype(BF)
    send_slots(lambda p2: rows(gx, p2 * 16, 16), rows(cxp, p * 16, 16), cx_s.at[0], cx_r.at[0])
    for n in range(2):
        gm[:, n * QD : (n + 1) * QD] = dot(table(z), tok[:, n * QD : (n + 1) * QD]).astype(BF)
        send_slots(
            lambda p2: half(gm, p2 * 16, 16, n), cot_half(z * ROWS + p * 16, 16, n), cm_s.at[n], cm_r.at[n]
        )

    def cot_block(zz, start, size):
        return cot.at[pl.ds(mult(zz * ROWS, 16), ROWS), cols(c * HD + start, size)]

    def to_sibling(zz):
        ref = cot_block(zz, 0, HD)
        remote(ref, ref, sib_s.at[zz], sib_r.at[zz], sib).start()

    drain(cxp, cx_r.at[0])
    place = (iota((EXT, MAIN), 0) // 4 == iota((EXT, MAIN), 1) // 16) & (
        iota((EXT, MAIN), 0) % 4 == iota((EXT, MAIN), 1) % 4
    )
    for q in range(4):
        unpack = one(place & ((iota((EXT, MAIN), 1) // 4) % 4 == q))
        cot[pl.ds(mult(z * ROWS + MAIN, 16), EXT), cols(c * HD + q * XD, XD)] = dot(
            unpack, cxp[...]
        ).astype(BF)
    for n in range(2):
        drain(cot_half(z * ROWS, MAIN, n), cm_r.at[n])
        ref = cot_block(z, n * QD, QD)
        remote(ref, ref, ag_s.at[2 * n], ag_r.at[2 * n], up).start()
        remote(ref, ref, ag_s.at[2 * n + 1], ag_r.at[2 * n + 1], down).start()
    to_sibling(z)

    drain(xh, hz_r.at[0])
    sx[...] = sum(
        dot(extra_pick(zz, zz), xh[(2 * zz + 1) * TOK : (2 * zz + 2) * TOK, :]) for zz in range(NZ)
    ).astype(BF)

    send_slots(lambda p2: rows(sx, p2 * 16, 16), rows(hxr, p * 16, 16), hm_s.at[4], hm_r.at[4])

    def order(k):
        return lax.rem(z + jnp.where(k == 2, 3, jnp.where(k == 3, 0, 2 - k)), 4)

    def pick_hidden(k, _):
        zz = order(k)
        at = pl.ds(mult(zz * MAIN, 16), MAIN)
        sm[at, :] = dot(table(zz), xh[at, :]).astype(BF)
        send_slots(
            lambda p2: rows(sm, zz * MAIN + p2 * 16, 16),
            rows(h, zz * ROWS + p * 16, 16),
            hm_s.at[zz],
            hm_r.at[zz],
        )
        return 0

    lax.fori_loop(0, NZ, pick_hidden, 0)

    drain(wv, w_sem.at[0])

    drain(hp.at[pl.ds(0, 7 * TOK)], hz_s.at[0])

    def slot_grads(zz):
        at = pl.ds(mult(zz * ROWS, 16), ROWS)
        hp[at, :] = dot_nt(cot[at, :], wv[...]).astype(BF)
        send_slots(
            lambda p2: rows(hp, zz * ROWS + p2 * 16, 16),
            rows(rm, zz * MAIN + p * 16, 16),
            ret_s.at[zz],
            ret_r.at[zz],
        )

    def other_half(zz):
        return cot.at[pl.ds(mult(zz * ROWS, 16), ROWS), cols(nc * HD, HD)]

    drain(other_half(z), sib_r.at[z])
    slot_grads(z)

    mine_out = pa

    def other_out(zz):
        return wg.at[pl.ds(mult(lax.div(zz, 2) * ROWS, 16), ROWS), cols(lax.rem(zz, 2) * HD, HD)]

    drain(hxr, hm_r.at[4])
    swap = one(
        (iota((MAIN, MAIN), 0) // 64 == (iota((MAIN, MAIN), 1) // 4) % 4)
        & ((iota((MAIN, MAIN), 0) // 4) % 16 == iota((MAIN, MAIN), 1) // 16)
        & (iota((MAIN, MAIN), 0) % 4 == iota((MAIN, MAIN), 1) % 4)
    )
    moved = dot(swap, hxr[...]).astype(BF)
    for zz in range(NZ):
        h[zz * ROWS + MAIN : (zz + 1) * ROWS, :] = moved[zz * EXT : (zz + 1) * EXT, :]

    def add_into(zz, start, size, ref):
        def step(i, _):
            at = pl.ds(mult(zz * ROWS + i * 32, 16), 32)
            where = cols(start, size)
            mine_out[at, where] = (
                mine_out[at, where].astype(F32) + ref(i)[...].astype(F32)
            ).astype(BF)
            return 0

        lax.fori_loop(0, ROWS // 32, step, 0)

    def add_cores(zz):
        drain(prcv.at[pl.ds(mult(zz * ROWS, 16), ROWS)], po_r.at[zz])
        add_into(zz, 0, HD, lambda i: prcv.at[pl.ds(mult(zz * ROWS + i * 32, 16), 32)])

    def sum_block(zz, n, s):
        return mine_out.at[pl.ds(mult(zz * ROWS, 16), ROWS), pl.ds(n * QD + s * XD, XD)]

    def r1_block(n, s):
        return r1.at[n, :, pl.ds(s * XD, XD)]

    def r2_block(side, n, s):
        return r2.at[side, :, pl.ds(n * QD + s * XD, XD)]

    def send_sum(src, dst, kind, s, dev):
        remote(src, dst, rs_s.at[2 * kind + s], rs_r.at[2 * kind + s], dev).start()

    def partials(k, _):
        zz = order(k)
        at = pl.ds(mult(zz * ROWS, 16), ROWS)

        @pl.when(k == 0)
        def _():
            drain(cot_block(zm, 0, QD), ag_r.at[0])
            ref = cot_block(zm, 0, QD)
            remote(ref, ref, agf_s.at[0], agf_r.at[0], up).start()
            drain(cot_block(zp, QD, QD), ag_r.at[3])
            ref2 = cot_block(zp, QD, QD)
            remote(ref2, ref2, agf_s.at[1], agf_r.at[1], down).start()

        drain(h.at[pl.ds(mult(zz * ROWS, 16), MAIN)], hm_r.at[zz])
        rows_in = h[at, :]

        def product(out, part):
            def tile(j, _):
                out[:, cols(j * QD, QD)] = dot(
                    rows_in, wv[:, cols(part * HD + j * QD, QD)]
                ).astype(BF)
                return 0

            lax.fori_loop(0, 2, tile, 0)

        product(other_out(zz), nc)
        remote(other_out(zz), prcv.at[at], po_s.at[zz], po_r.at[zz], sib).start()
        product(mine_out.at[at], c)

        @pl.when(k == 1)
        def _():
            add_cores(zo)
            for s in range(2):
                send_sum(sum_block(zo, 0, s), r1_block(0, s), 0, s, up)
                send_sum(sum_block(zo, 1, s), r1_block(1, s), 1, s, down)

        @pl.when(k == 2)
        def _():
            add_cores(zp)
            for s in range(2):
                send_sum(sum_block(zp, 1, s), r2_block(0, 1, s), 2, s, up)
            drain(cot_block(zm, QD, QD), ag_r.at[2])
            to_sibling(zm)
            drain(cot_block(zp, 0, QD), ag_r.at[1])
            to_sibling(zp)

        @pl.when(k == 3)
        def _():
            add_cores(zm)
            for s in range(2):
                send_sum(sum_block(zm, 0, s), r2_block(1, 0, s), 3, s, down)

        return 0

    lax.fori_loop(0, NZ, partials, 0)
    add_cores(z)

    def more_grads(k, _):
        zz = lax.rem(z + jnp.where(k == 0, 1, jnp.where(k == 1, 3, 2)), 4)

        @pl.when(k == 2)
        def _():
            drain(cot_block(zo, 0, QD), agf_r.at[0])
            drain(cot_block(zo, QD, QD), agf_r.at[1])
            to_sibling(zo)

        drain(other_half(zz), sib_r.at[zz])
        slot_grads(zz)
        return 0

    lax.fori_loop(0, 3, more_grads, 0)

    unswap = one(
        (iota((MAIN, MAIN), 1) // 64 == (iota((MAIN, MAIN), 0) // 4) % 4)
        & ((iota((MAIN, MAIN), 1) // 4) % 16 == iota((MAIN, MAIN), 0) // 16)
        & (iota((MAIN, MAIN), 1) % 4 == iota((MAIN, MAIN), 0) % 4)
    )
    drain(hp.at[pl.ds(0, 240)], hm_s.at[4])
    hpx[...] = sum(
        dot(unswap[:, zz * EXT : (zz + 1) * EXT], hp[zz * ROWS + MAIN : (zz + 1) * ROWS, :])
        for zz in range(NZ)
    ).astype(BF)
    send_slots(lambda p2: rows(hpx, p2 * 16, 16), rows(rx, p * 16, 16), ret_s.at[4], ret_r.at[4])

    for s in range(2):
        for n, zz, dev in ((0, zp, up), (1, zm, down)):
            drain(r1_block(n, s), rs_r.at[2 * n + s])
            add_into(
                zz,
                n * QD + s * XD,
                XD,
                lambda i: r1.at[n, pl.ds(mult(i * 32, 16), 32), pl.ds(s * XD, XD)],
            )
            send_sum(sum_block(zz, n, s), r2_block(n, n, s), 4 + n, s, dev)

    for zz in range(NZ):
        drain(prcv.at[0:ROWS], po_s.at[zz])

    def weight_grads(j, _):
        at = cols(j * XD, XD)
        wg[:, at] = dot_tn(h[...], cot[:, at]).astype(BF)
        return 0

    lax.fori_loop(0, 8, weight_grads, 0)

    drain(rx, ret_r.at[4])

    def tokens_grad(zz, _):
        at = pl.ds(mult(zz * MAIN, 16), MAIN)
        drain(rm.at[at], ret_r.at[zz])
        grads = dot_tn(table(zz), rm[at, :])
        late = dot_tn(extra_pick(zz, zz), rx[...])
        xh[pl.ds(mult(zz * MAIN, 16), TOK), :] = grads[0:TOK, :].astype(BF)
        xh[pl.ds(mult(zz * MAIN + TOK, 16), TOK), :] = (grads[TOK:, :] + late).astype(BF)
        return 0

    lax.fori_loop(0, NZ, tokens_grad, 0)

    for n in range(2):
        drain(half(gm, 0, 240, n), cm_s.at[n])
    drain(gx.at[pl.ds(0, 240)], cx_s.at[0])

    def return_grads(piece):
        for dc, dz in COLUMN:
            c2, z2, dev = column(dc, dz)
            src = rows(xh, (z2 * 2 + c2) * TOK + piece * 32, 32)
            dst = hg.at[pl.ds(mult(piece * 32, 16), 32), cols(blk * FB, FB)]
            remote(src, dst, hg_s.at[0], hg_r.at[0], dev).start()

    def last_sum(first, count, n, s):
        at = pl.ds(mult(z * ROWS + first, 16), count)
        there = pl.ds(mult(first, 16), count)
        where = pl.ds(n * QD + s * XD, XD)
        return (
            mine_out[at, where].astype(F32)
            + r2[0, there, where].astype(F32)
            + r2[1, there, where].astype(F32)
        ).astype(BF)

    back = (iota((MAIN, EXT), 1) // 4 == iota((MAIN, EXT), 0) // 16) & (
        iota((MAIN, EXT), 1) % 4 == iota((MAIN, EXT), 0) % 4
    )
    SD = XD // 2
    for s in range(2):
        for kind, side, n in ((2, 0, 1), (3, 1, 0), (4, 0, 0), (5, 1, 1)):
            drain(r2_block(side, n, s), rs_r.at[2 * kind + s])
        if s == 1:
            lax.fori_loop(0, 4, lambda piece, _: return_grads(piece) or 0, 0)
        for n in range(2):

            def main_rows(i, _):
                at = pl.ds(mult(i * 32, 16), 32)
                gm[at, (2 * s + n) * XD : (2 * s + n + 1) * XD] = last_sum(i * 32, 32, n, s)
                return 0

            lax.fori_loop(0, MAIN // 32, main_rows, 0)
        send_slots(
            lambda p2: half(gm, p2 * 16, 16, s), half(em, p * 16, 16, s), eo_s.at[s], eo_r.at[s]
        )
        tails = [last_sum(MAIN, EXT, n, s) for n in range(2)]
        ex[:, s * SD : (s + 1) * SD] = sum(
            dot(
                one(back & ((iota((MAIN, EXT), 0) // 4) % 4 == q)),
                tails[q // 2][:, (q % 2) * SD : (q % 2 + 1) * SD],
            )
            for q in range(4)
        ).astype(BF)
        send_slots(
            lambda p2: ex.at[pl.ds(mult(p2 * 16, 16), 16), pl.ds(s * SD, SD)],
            exr.at[pl.ds(mult(p * 16, 16), 16), pl.ds(s * SD, SD)],
            eo_s.at[2 + s],
            eo_r.at[2 + s],
        )
    local(rows(xh, (z * 2 + c) * TOK, TOK), hg.at[:, cols(blk * FB, FB)], hg_r.at[0]).start()

    for s in range(2):
        drain(half(em, 0, MAIN, s), eo_r.at[s])
        drain(exr.at[:, pl.ds(s * SD, SD)], eo_r.at[2 + s])
        rows_out = dot_tn(table(z), em[:, s * QD : (s + 1) * QD])
        late = jnp.concatenate(
            [dot_tn(extra_pick(z, q), exr[:, s * SD : (s + 1) * SD]) for q in range(4)], axis=1
        )
        kk[0:TOK, s * QD : (s + 1) * QD] = rows_out[0:TOK, :].astype(BF)
        kk[TOK : 2 * TOK, s * QD : (s + 1) * QD] = (rows_out[TOK:, :] + late).astype(BF)
        for n in range(2):
            m = 2 * s + n
            there = picked.at[:, cols(c * HD + n * QD + s * XD, XD)]
            src = kk.at[pl.ds(mult(nc * TOK, 16), TOK), pl.ds(m * XD, XD)]
            remote(src, there, k_s.at[m], k_r.at[m], sib).start()
            src = kk.at[pl.ds(mult(c * TOK, 16), TOK), pl.ds(m * XD, XD)]
            local(src, there, k_s.at[4 + m]).start()

    for m in range(4):
        there = picked.at[:, cols(nc * HD + (m % 2) * QD + (m // 2) * XD, XD)]
        drain(there, k_r.at[m])
        drain(there, k_s.at[m])
        drain(there, k_s.at[4 + m])
    drain(hg, hg_r.at[0])
    drain(rows(posv, 0, 56, 8), pos_s.at[0])
    drain(xh.at[pl.ds(0, 7 * TOK)], hg_s.at[0])
    drain(tsend, t_s.at[0])
    for s in range(2):
        drain(half(em, 0, 240, s), eo_s.at[s])
        drain(exr.at[pl.ds(0, 240), pl.ds(s * SD, SD)], eo_s.at[2 + s])
    for n in range(5):
        if n < 4:
            drain(hp.at[pl.ds(0, 240)], hm_s.at[n])
        drain(hp.at[pl.ds(0, 240)], ret_s.at[n])
    for n in range(4):
        drain(r1.at[0], ag_s.at[n])
        drain(r2.at[0], sib_s.at[n])
    for n in range(2):
        drain(r1.at[0], agf_s.at[n])
    for n in range(12):
        drain(r1_block(0, 0), rs_s.at[n])


PIECES = 4


def finish(picked, gates, og_hbm, hg_in, wg_in, mixed, hg, wg, gg, og, out, in_sem, out_sem):
    load = pltpu.make_async_copy(og_hbm, og, in_sem.at[0])
    load.start()
    stores = [pltpu.make_async_copy(hg_in, hg, out_sem.at[PIECES])]
    for k in range(PIECES):
        at = pl.ds(k * (FB // PIECES), FB // PIECES)
        stores.append(pltpu.make_async_copy(wg_in.at[at], wg.at[at], out_sem.at[k]))
    for copy in stores:
        copy.start()
    eye = iota((TOK, TOK), 0) == iota((TOK, TOK), 1)
    gate = jnp.sum(jnp.where(eye, gates[...], 0.0), axis=1, keepdims=True)
    rows = picked[...].astype(F32)
    out[...] = (gate * rows).astype(BF)
    stores.append(pltpu.make_async_copy(out, mixed, out_sem.at[PIECES + 1]))
    stores[-1].start()
    load.wait()
    total = jnp.sum(og[...].astype(F32) * rows, axis=1, keepdims=True)
    gg[...] = jnp.sum(jnp.where(eye, total, 0.0), axis=0, keepdims=True)
    for copy in stores:
        copy.wait()


def layer(hidden_in, weights, gates, group_ids, slot_ids, out_grad):
    vmem = pl.BlockSpec(memory_space=pltpu.VMEM)
    anywhere = pl.BlockSpec(memory_space=pl.ANY)
    sem = pltpu.SemaphoreType.DMA

    def buf(*shape):
        return pltpu.VMEM(shape, BF)

    gate_row = gates.reshape(1, TOK)
    picked, hidden_grad, weight_grad = pl.pallas_call(
        kernel,
        out_shape=(pltpu.VMEM((TOK, D), BF), pltpu.VMEM((TOK, FF), BF), pltpu.VMEM((FB, D), BF)),
        in_specs=[anywhere, anywhere, vmem, vmem, vmem, anywhere],
        out_specs=(vmem, vmem, vmem),
        scratch_shapes=[
            buf(FB, D),
            buf(NZ * ROWS, FB),
            buf(MAIN, FB),
            buf(NZ * ROWS, D),
            buf(MAIN, XD),
            buf(8 * TOK, FB),
            buf(NZ * MAIN, FB),
            buf(MAIN, FB),
            buf(2 * TOK, HD),
            buf(TOK, HD),
            buf(MAIN, HD),
            buf(MAIN, XD),
            buf(NZ * ROWS, HD),
            buf(NZ * ROWS, HD),
            buf(2, ROWS, QD),
            buf(2, ROWS, HD),
            buf(MAIN, HD),
            buf(MAIN, XD),
            buf(NZ * ROWS, FB),
            buf(NZ * MAIN, FB),
            buf(MAIN, FB),
            buf(TOK, D),
            buf(NZ * MAIN, 2 * TOK),
            buf(NZ * MAIN, TOK),
            pltpu.VMEM((8 * 8, TOK), jnp.int32),
            sem((1,)), sem((1,)),
            sem((1,)), sem((1,)),
            sem((1,)), sem((1,)), sem((1,)),
            sem((1,)), sem((1,)),
            sem((2,)), sem((2,)),
            sem((1,)), sem((1,)),
            sem((5,)), sem((5,)),
            sem((4,)), sem((4,)),
            sem((2,)), sem((2,)),
            sem((4,)), sem((4,)),
            sem((4,)), sem((4,)),
            sem((12,)), sem((12,)),
            sem((5,)), sem((5,)),
            sem((4,)), sem((4,)),
            sem((8,)), sem((4,)),
            sem((1,)), sem((1,)),
        ],
        compiler_params=pltpu.CompilerParams(
            collective_id=0, has_side_effects=True, vmem_limit_bytes=54 * 1024 * 1024 - 65536
        ),
        cost_estimate=pl.CostEstimate(
            flops=6 * NZ * ROWS * FB * D, bytes_accessed=20_000_000, transcendentals=0
        ),
        name="experts",
    )(hidden_in, weights, gate_row, group_ids.reshape(1, TOK), slot_ids.reshape(1, TOK), out_grad)

    results = [
        pltpu.with_memory_space_constraint(value, pltpu.VMEM)
        for value in (picked, hidden_grad, weight_grad)
    ]
    mixed, hidden_grad, weight_grad, gate_grad = pl.pallas_call(
        finish,
        out_shape=(
            jax.ShapeDtypeStruct((TOK, D), BF),
            jax.ShapeDtypeStruct((TOK, FF), BF),
            jax.ShapeDtypeStruct((FB, D), BF),
            jax.ShapeDtypeStruct((1, TOK), F32),
        ),
        in_specs=[vmem, vmem, anywhere, vmem, vmem],
        out_specs=(anywhere, anywhere, anywhere, vmem),
        scratch_shapes=[buf(TOK, D), buf(TOK, D), sem((1,)), sem((PIECES + 2,))],
        compiler_params=pltpu.CompilerParams(vmem_limit_bytes=52 * 1024 * 1024),
        name="finish",
    )(results[0], gate_row, out_grad, results[1], results[2])
    return mixed, hidden_grad, weight_grad, gate_grad.reshape(TOK)


def solution(mesh):
    wide, flat = P(("grp", "exp"), None), P(("grp", "exp"))
    return jax.shard_map(
        layer,
        mesh=mesh,
        in_specs=(wide, wide, flat, flat, flat, wide),
        out_specs=(wide, wide, wide, flat),
        check_vma=False,
    )
```

```python
import functools

import jax
import jax.numpy as jnp
from jax import lax
from jax.experimental import pallas as pl
from jax.experimental.pallas import tpu as pltpu
from jax.sharding import PartitionSpec as P

MESH = pl.DeviceIdType.MESH
BF = jnp.bfloat16
F32 = jnp.float32
TOK, CAP = 128, 10
D, FF, FB = 4096, 7168, 896
HD, QD, XD = D // 2, D // 4, D // 8
NP, NZ = 16, 4
MAIN, EXT, ROWS = 256, 64, 320


def hops(k):
    return min(k, 4 - k)


PLANE = sorted(
    [(i, j) for i in range(4) for j in range(4) if i + j], key=lambda o: -(hops(o[0]) + hops(o[1]))
)
COLUMN = [(0, 2), (1, 2), (0, 1), (0, 3), (1, 1), (1, 3), (1, 0)]


def dot(a, b, dims=((1,), (0,))):
    return lax.dot_general(a, b, (dims, ((), ())), preferred_element_type=F32)


def dot_tn(a, b):
    return dot(a, b, ((0,), (0,)))


def dot_nt(a, b):
    return dot(a, b, ((1,), (1,)))


def one(cond):
    return jnp.where(cond, 1.0, 0.0).astype(F32).astype(BF)


def iota(shape, dim):
    return lax.broadcasted_iota(jnp.int32, shape, dim)


def mult(value, of):
    return pl.multiple_of(value, of)


def kernel(
    hid, w_hbm, gates, group_ids, slot_ids, og_hbm,
    mixed, hg, wg, gg,
    wv, h, hxr, cot, cxp, xh, sm, sx, tok, tsend, gm, gx, pa, prcv, r1, r2, hp, rm, rx, kr, og,
    mt, xb, posv,
    pos_s, pos_r, hz_s, hz_r, w_sem, og_sem, st_sem, t_s, t_r, cm_s, cm_r, cx_s, cx_r, hm_s, hm_r,
    ag_s, ag_r, agf_s, agf_r, sib_s, sib_r, po_s, po_r, rs_s, rs_r, ret_s, ret_r, eo_s, eo_r, k_s, k_r, hg_s, hg_r,
):
    g = lax.axis_index("grp")
    z = lax.axis_index("exp")
    c = lax.rem(g, 2)
    p = lax.div(g, 2)
    x = lax.div(p, 4)
    y = lax.rem(p, 4)
    nc = 1 - c
    zp = lax.rem(z + 1, 4)
    zm = lax.rem(z + 3, 4)
    zo = lax.rem(z + 2, 4)
    sib = (p * 2 + nc, z)
    up = (g, zp)
    down = (g, zm)
    blk = c * 4 + z
    kk, hpx, ex, em, exr = prcv, sx, gx, tok, cxp

    def plane(i, j):
        p2 = lax.rem(x + i, 4) * 4 + lax.rem(y + j, 4)
        return p2, (p2 * 2 + c, z)

    def column(dc, dz):
        c2 = lax.rem(c + dc, 2)
        z2 = lax.rem(z + dz, 4)
        return c2, z2, (p * 2 + c2, z2)

    def remote(src, dst, ss, rs, dev):
        return pltpu.make_async_remote_copy(
            src_ref=src, dst_ref=dst, send_sem=ss, recv_sem=rs, device_id=dev, device_id_type=MESH
        )

    def local(src, dst, sem):
        return pltpu.make_async_copy(src, dst, sem)

    def drain(ref, sem):
        pltpu.make_async_copy(ref, ref, sem).wait()

    def rows(ref, start, size, of=16):
        return ref.at[pl.ds(mult(start, of), size)]

    def cols(start, size):
        return pl.ds(mult(start, 128), size)

    barrier = pltpu.get_barrier_semaphore()
    for dc, dz in COLUMN:
        pl.semaphore_signal(barrier, inc=1, device_id=column(dc, dz)[2], device_id_type=MESH)
    for i, j in PLANE:
        pl.semaphore_signal(barrier, inc=1, device_id=plane(i, j)[1], device_id_type=MESH)

    local(og_hbm, og, og_sem.at[0]).start()
    for k in range(8):
        local(hid.at[:, pl.ds(k * FB, FB)], hp.at[pl.ds(k * TOK, TOK)], st_sem.at[0]).start()
    local(w_hbm, wv, w_sem.at[0]).start()
    position = group_ids[...] * CAP + slot_ids[...]
    posv[pl.ds(mult((z * 2 + c) * 8, 8), 8), :] = jnp.broadcast_to(position, (8, TOK))
    eye = iota((TOK, TOK), 0) == iota((TOK, TOK), 1)
    gate = jnp.sum(jnp.where(eye, gates[...], 0.0), axis=1, keepdims=True)
    drain(og, og_sem.at[0])
    tsend[...] = (gate * og[:, cols(nc * HD, HD)].astype(F32)).astype(BF)
    drain(hp.at[pl.ds(0, 8 * TOK)], st_sem.at[0])
    pl.semaphore_wait(barrier, len(COLUMN) + len(PLANE))

    remote(tsend, rows(tok, c * TOK, TOK), t_s.at[0], t_r.at[0], sib).start()
    mine = rows(posv, (z * 2 + c) * 8, 8, 8)
    for dc, dz in COLUMN:
        remote(mine, mine, pos_s.at[0], pos_r.at[0], column(dc, dz)[2]).start()

    def send_hidden(piece, _):
        for dc, dz in COLUMN:
            c2, z2, dev = column(dc, dz)
            src = rows(hp, (c2 * 4 + z2) * TOK + piece * 32, 32)
            dst = rows(xh, (z * 2 + c) * TOK + piece * 32, 32)
            remote(src, dst, hz_s.at[0], hz_r.at[0], dev).start()
        return 0

    lax.fori_loop(0, 4, send_hidden, 0)
    local(rows(hp, blk * TOK, TOK), rows(xh, (z * 2 + c) * TOK, TOK), hz_r.at[0]).start()
    tok[pl.ds(mult(c * TOK, 16), TOK), :] = (gate * og[:, cols(c * HD, HD)].astype(F32)).astype(BF)

    drain(rows(posv, 0, 56, 8), pos_r.at[0])

    def tables(zz, _):
        group = iota((MAIN, TOK), 0) // 16
        slot = iota((MAIN, TOK), 0) % 16
        both = posv[pl.ds(mult(zz * 16, 16), 16), :]
        first, second = both[0:1, :], both[8:9, :]
        at = pl.ds(mult(zz * MAIN, 16), MAIN)
        mt[at, 0:TOK] = one((slot < CAP) & (group * CAP + slot == first))
        mt[at, TOK : 2 * TOK] = one((slot >= CAP) & (group * CAP + slot - CAP == second))
        xb[at, :] = one(group * CAP + slot % 4 + 6 == second)
        return 0

    lax.fori_loop(0, NZ, tables, 0)
    part = (iota((MAIN, TOK), 0) // 4) % 4

    def extra_pick(zz, q):
        base = xb[pl.ds(mult(zz * MAIN, 16), MAIN), :]
        return jnp.where(part == q, base.astype(F32), 0.0).astype(BF)

    def table(zz):
        return mt[pl.ds(mult(zz * MAIN, 16), MAIN), :]

    def half(ref, start, size, n):
        return ref.at[pl.ds(mult(start, 16), size), pl.ds(n * QD, QD)]

    def cot_half(start, size, n):
        return cot.at[pl.ds(mult(start, 16), size), cols(c * HD + n * QD, QD)]

    def send_slots(src, dst, ss, rs):
        for i, j in PLANE:
            p2, dev = plane(i, j)
            remote(src(p2), dst, ss, rs, dev).start()
        local(src(p), dst, rs).start()

    drain(tsend, t_r.at[0])
    gx[...] = sum(
        dot(extra_pick(z, q), tok[TOK : 2 * TOK, q * XD : (q + 1) * XD]) for q in range(4)
    ).astype(BF)
    send_slots(lambda p2: rows(gx, p2 * 16, 16), rows(cxp, p * 16, 16), cx_s.at[0], cx_r.at[0])
    for n in range(2):
        gm[:, n * QD : (n + 1) * QD] = dot(table(z), tok[:, n * QD : (n + 1) * QD]).astype(BF)
        send_slots(
            lambda p2: half(gm, p2 * 16, 16, n), cot_half(z * ROWS + p * 16, 16, n), cm_s.at[n], cm_r.at[n]
        )

    def cot_block(zz, start, size):
        return cot.at[pl.ds(mult(zz * ROWS, 16), ROWS), cols(c * HD + start, size)]

    def to_sibling(zz):
        ref = cot_block(zz, 0, HD)
        remote(ref, ref, sib_s.at[zz], sib_r.at[zz], sib).start()

    drain(cxp, cx_r.at[0])
    place = (iota((EXT, MAIN), 0) // 4 == iota((EXT, MAIN), 1) // 16) & (
        iota((EXT, MAIN), 0) % 4 == iota((EXT, MAIN), 1) % 4
    )
    for q in range(4):
        unpack = one(place & ((iota((EXT, MAIN), 1) // 4) % 4 == q))
        cot[pl.ds(mult(z * ROWS + MAIN, 16), EXT), cols(c * HD + q * XD, XD)] = dot(
            unpack, cxp[...]
        ).astype(BF)
    for n in range(2):
        drain(cot_half(z * ROWS, MAIN, n), cm_r.at[n])
        ref = cot_block(z, n * QD, QD)
        remote(ref, ref, ag_s.at[2 * n], ag_r.at[2 * n], up).start()
        remote(ref, ref, ag_s.at[2 * n + 1], ag_r.at[2 * n + 1], down).start()
    to_sibling(z)

    drain(xh, hz_r.at[0])
    sx[...] = sum(
        dot(extra_pick(zz, zz), xh[(2 * zz + 1) * TOK : (2 * zz + 2) * TOK, :]) for zz in range(NZ)
    ).astype(BF)

    send_slots(lambda p2: rows(sx, p2 * 16, 16), rows(hxr, p * 16, 16), hm_s.at[4], hm_r.at[4])

    def order(k):
        return lax.rem(z + jnp.where(k == 2, 3, jnp.where(k == 3, 0, 2 - k)), 4)

    def pick_hidden(k, _):
        zz = order(k)
        at = pl.ds(mult(zz * MAIN, 16), MAIN)
        sm[at, :] = dot(table(zz), xh[at, :]).astype(BF)
        send_slots(
            lambda p2: rows(sm, zz * MAIN + p2 * 16, 16),
            rows(h, zz * ROWS + p * 16, 16),
            hm_s.at[zz],
            hm_r.at[zz],
        )
        return 0

    lax.fori_loop(0, NZ, pick_hidden, 0)

    drain(wv, w_sem.at[0])

    drain(hp.at[pl.ds(0, 7 * TOK)], hz_s.at[0])

    def slot_grads(zz):
        at = pl.ds(mult(zz * ROWS, 16), ROWS)
        hp[at, :] = dot_nt(cot[at, :], wv[...]).astype(BF)
        send_slots(
            lambda p2: rows(hp, zz * ROWS + p2 * 16, 16),
            rows(rm, zz * MAIN + p * 16, 16),
            ret_s.at[zz],
            ret_r.at[zz],
        )

    def other_half(zz):
        return cot.at[pl.ds(mult(zz * ROWS, 16), ROWS), cols(nc * HD, HD)]

    drain(other_half(z), sib_r.at[z])
    slot_grads(z)

    mine_out = pa

    def other_out(zz):
        return wg.at[pl.ds(mult(lax.div(zz, 2) * ROWS, 16), ROWS), cols(lax.rem(zz, 2) * HD, HD)]

    drain(hxr, hm_r.at[4])
    swap = one(
        (iota((MAIN, MAIN), 0) // 64 == (iota((MAIN, MAIN), 1) // 4) % 4)
        & ((iota((MAIN, MAIN), 0) // 4) % 16 == iota((MAIN, MAIN), 1) // 16)
        & (iota((MAIN, MAIN), 0) % 4 == iota((MAIN, MAIN), 1) % 4)
    )
    moved = dot(swap, hxr[...]).astype(BF)
    for zz in range(NZ):
        h[zz * ROWS + MAIN : (zz + 1) * ROWS, :] = moved[zz * EXT : (zz + 1) * EXT, :]

    def add_into(zz, start, size, ref):
        def step(i, _):
            at = pl.ds(mult(zz * ROWS + i * 32, 16), 32)
            where = cols(start, size)
            mine_out[at, where] = (
                mine_out[at, where].astype(F32) + ref(i)[...].astype(F32)
            ).astype(BF)
            return 0

        lax.fori_loop(0, ROWS // 32, step, 0)

    def add_cores(zz):
        drain(prcv.at[pl.ds(mult(zz * ROWS, 16), ROWS)], po_r.at[zz])
        add_into(zz, 0, HD, lambda i: prcv.at[pl.ds(mult(zz * ROWS + i * 32, 16), 32)])

    def sum_block(zz, n, s):
        return mine_out.at[pl.ds(mult(zz * ROWS, 16), ROWS), pl.ds(n * QD + s * XD, XD)]

    def r1_block(n, s):
        return r1.at[n, :, pl.ds(s * XD, XD)]

    def r2_block(side, n, s):
        return r2.at[side, :, pl.ds(n * QD + s * XD, XD)]

    def send_sum(src, dst, kind, s, dev):
        remote(src, dst, rs_s.at[2 * kind + s], rs_r.at[2 * kind + s], dev).start()

    def partials(k, _):
        zz = order(k)
        at = pl.ds(mult(zz * ROWS, 16), ROWS)

        @pl.when(k == 0)
        def _():
            drain(cot_block(zm, 0, QD), ag_r.at[0])
            ref = cot_block(zm, 0, QD)
            remote(ref, ref, agf_s.at[0], agf_r.at[0], up).start()
            drain(cot_block(zp, QD, QD), ag_r.at[3])
            ref2 = cot_block(zp, QD, QD)
            remote(ref2, ref2, agf_s.at[1], agf_r.at[1], down).start()

        drain(h.at[pl.ds(mult(zz * ROWS, 16), MAIN)], hm_r.at[zz])
        rows_in = h[at, :]

        def product(out, part):
            def tile(j, _):
                out[:, cols(j * QD, QD)] = dot(
                    rows_in, wv[:, cols(part * HD + j * QD, QD)]
                ).astype(BF)
                return 0

            lax.fori_loop(0, 2, tile, 0)

        product(other_out(zz), nc)
        remote(other_out(zz), prcv.at[at], po_s.at[zz], po_r.at[zz], sib).start()
        product(mine_out.at[at], c)

        @pl.when(k == 1)
        def _():
            add_cores(zo)
            for s in range(2):
                send_sum(sum_block(zo, 0, s), r1_block(0, s), 0, s, up)
                send_sum(sum_block(zo, 1, s), r1_block(1, s), 1, s, down)

        @pl.when(k == 2)
        def _():
            add_cores(zp)
            for s in range(2):
                send_sum(sum_block(zp, 1, s), r2_block(0, 1, s), 2, s, up)
            drain(cot_block(zm, QD, QD), ag_r.at[2])
            to_sibling(zm)
            drain(cot_block(zp, 0, QD), ag_r.at[1])
            to_sibling(zp)

        @pl.when(k == 3)
        def _():
            add_cores(zm)
            for s in range(2):
                send_sum(sum_block(zm, 0, s), r2_block(1, 0, s), 3, s, down)

        return 0

    lax.fori_loop(0, NZ, partials, 0)
    add_cores(z)

    def more_grads(k, _):
        zz = lax.rem(z + jnp.where(k == 0, 1, jnp.where(k == 1, 3, 2)), 4)

        @pl.when(k == 2)
        def _():
            drain(cot_block(zo, 0, QD), agf_r.at[0])
            drain(cot_block(zo, QD, QD), agf_r.at[1])
            to_sibling(zo)

        drain(other_half(zz), sib_r.at[zz])
        slot_grads(zz)
        return 0

    lax.fori_loop(0, 3, more_grads, 0)

    unswap = one(
        (iota((MAIN, MAIN), 1) // 64 == (iota((MAIN, MAIN), 0) // 4) % 4)
        & ((iota((MAIN, MAIN), 1) // 4) % 16 == iota((MAIN, MAIN), 0) // 16)
        & (iota((MAIN, MAIN), 1) % 4 == iota((MAIN, MAIN), 0) % 4)
    )
    drain(hp.at[pl.ds(0, 240)], hm_s.at[4])
    hpx[...] = sum(
        dot(unswap[:, zz * EXT : (zz + 1) * EXT], hp[zz * ROWS + MAIN : (zz + 1) * ROWS, :])
        for zz in range(NZ)
    ).astype(BF)
    send_slots(lambda p2: rows(hpx, p2 * 16, 16), rows(rx, p * 16, 16), ret_s.at[4], ret_r.at[4])

    for s in range(2):
        for n, zz, dev in ((0, zp, up), (1, zm, down)):
            drain(r1_block(n, s), rs_r.at[2 * n + s])
            add_into(
                zz,
                n * QD + s * XD,
                XD,
                lambda i: r1.at[n, pl.ds(mult(i * 32, 16), 32), pl.ds(s * XD, XD)],
            )
            send_sum(sum_block(zz, n, s), r2_block(n, n, s), 4 + n, s, dev)

    for zz in range(NZ):
        drain(prcv.at[0:ROWS], po_s.at[zz])

    def weight_grads(j, _):
        at = cols(j * XD, XD)
        wg[:, at] = dot_tn(h[...], cot[:, at]).astype(BF)
        return 0

    lax.fori_loop(0, 8, weight_grads, 0)

    drain(rx, ret_r.at[4])

    def tokens_grad(zz, _):
        at = pl.ds(mult(zz * MAIN, 16), MAIN)
        drain(rm.at[at], ret_r.at[zz])
        grads = dot_tn(table(zz), rm[at, :])
        late = dot_tn(extra_pick(zz, zz), rx[...])
        xh[pl.ds(mult(zz * MAIN, 16), TOK), :] = grads[0:TOK, :].astype(BF)
        xh[pl.ds(mult(zz * MAIN + TOK, 16), TOK), :] = (grads[TOK:, :] + late).astype(BF)
        return 0

    lax.fori_loop(0, NZ, tokens_grad, 0)

    for n in range(2):
        drain(half(gm, 0, 240, n), cm_s.at[n])
    drain(gx.at[pl.ds(0, 240)], cx_s.at[0])

    def return_grads(piece):
        for dc, dz in COLUMN:
            c2, z2, dev = column(dc, dz)
            src = rows(xh, (z2 * 2 + c2) * TOK + piece * 32, 32)
            dst = hg.at[pl.ds(mult(piece * 32, 16), 32), cols(blk * FB, FB)]
            remote(src, dst, hg_s.at[0], hg_r.at[0], dev).start()

    def last_sum(first, count, n, s):
        at = pl.ds(mult(z * ROWS + first, 16), count)
        there = pl.ds(mult(first, 16), count)
        where = pl.ds(n * QD + s * XD, XD)
        return (
            mine_out[at, where].astype(F32)
            + r2[0, there, where].astype(F32)
            + r2[1, there, where].astype(F32)
        ).astype(BF)

    back = (iota((MAIN, EXT), 1) // 4 == iota((MAIN, EXT), 0) // 16) & (
        iota((MAIN, EXT), 1) % 4 == iota((MAIN, EXT), 0) % 4
    )
    SD = XD // 2
    for s in range(2):
        for kind, side, n in ((2, 0, 1), (3, 1, 0), (4, 0, 0), (5, 1, 1)):
            drain(r2_block(side, n, s), rs_r.at[2 * kind + s])
        lax.fori_loop(2 * s, 2 + 2 * s, lambda piece, _: return_grads(piece) or 0, 0)
        for n in range(2):

            def main_rows(i, _):
                at = pl.ds(mult(i * 32, 16), 32)
                gm[at, (2 * s + n) * XD : (2 * s + n + 1) * XD] = last_sum(i * 32, 32, n, s)
                return 0

            lax.fori_loop(0, MAIN // 32, main_rows, 0)
        send_slots(
            lambda p2: half(gm, p2 * 16, 16, s), half(em, p * 16, 16, s), eo_s.at[s], eo_r.at[s]
        )
        tails = [last_sum(MAIN, EXT, n, s) for n in range(2)]
        ex[:, s * SD : (s + 1) * SD] = sum(
            dot(
                one(back & ((iota((MAIN, EXT), 0) // 4) % 4 == q)),
                tails[q // 2][:, (q % 2) * SD : (q % 2 + 1) * SD],
            )
            for q in range(4)
        ).astype(BF)
        send_slots(
            lambda p2: ex.at[pl.ds(mult(p2 * 16, 16), 16), pl.ds(s * SD, SD)],
            exr.at[pl.ds(mult(p * 16, 16), 16), pl.ds(s * SD, SD)],
            eo_s.at[2 + s],
            eo_r.at[2 + s],
        )
    local(rows(xh, (z * 2 + c) * TOK, TOK), hg.at[:, cols(blk * FB, FB)], hg_r.at[0]).start()

    for s in range(2):
        drain(half(em, 0, MAIN, s), eo_r.at[s])
        drain(exr.at[:, pl.ds(s * SD, SD)], eo_r.at[2 + s])
        rows_out = dot_tn(table(z), em[:, s * QD : (s + 1) * QD])
        late = jnp.concatenate(
            [dot_tn(extra_pick(z, q), exr[:, s * SD : (s + 1) * SD]) for q in range(4)], axis=1
        )
        kk[0:TOK, s * QD : (s + 1) * QD] = rows_out[0:TOK, :].astype(BF)
        kk[TOK : 2 * TOK, s * QD : (s + 1) * QD] = (rows_out[TOK:, :] + late).astype(BF)
        src = kk.at[pl.ds(mult(nc * TOK, 16), TOK), pl.ds(s * QD, QD)]
        remote(src, kr.at[:, pl.ds(s * QD, QD)], k_s.at[s], k_r.at[s], sib).start()

    total = jnp.zeros((TOK, 1), F32)
    for core, ref, first in ((c, kk, mult(c * TOK, 16)), (nc, kr, 0)):
        for s in range(2):
            if ref is kr:
                drain(kr.at[:, pl.ds(s * QD, QD)], k_r.at[s])
            for n in range(2):
                at = cols(core * HD + n * QD + s * XD, XD)
                picked = ref[pl.ds(first, TOK), (2 * s + n) * XD : (2 * s + n + 1) * XD].astype(F32)
                total += jnp.sum(og[:, at].astype(F32) * picked, axis=1, keepdims=True)
                mixed[:, at] = (gate * picked).astype(BF)
    gg[...] = jnp.sum(jnp.where(eye, total, 0.0), axis=0, keepdims=True)

    for s in range(2):
        drain(kr.at[:, pl.ds(s * QD, QD)], k_s.at[s])
    drain(hg, hg_r.at[0])
    drain(rows(posv, 0, 56, 8), pos_s.at[0])
    drain(xh.at[pl.ds(0, 7 * TOK)], hg_s.at[0])
    drain(tsend, t_s.at[0])
    for s in range(2):
        drain(half(em, 0, 240, s), eo_s.at[s])
        drain(exr.at[pl.ds(0, 240), pl.ds(s * SD, SD)], eo_s.at[2 + s])
    for n in range(5):
        if n < 4:
            drain(hp.at[pl.ds(0, 240)], hm_s.at[n])
        drain(hp.at[pl.ds(0, 240)], ret_s.at[n])
    for n in range(4):
        drain(r1.at[0], ag_s.at[n])
        drain(r2.at[0], sib_s.at[n])
    for n in range(2):
        drain(r1.at[0], agf_s.at[n])
    for n in range(12):
        drain(r1_block(0, 0), rs_s.at[n])


PIECES = 4


def finish(mixed_in, hg_in, wg_in, gg_in, mixed, hg, wg, gg, sems):
    copies = [(mixed_in, mixed), (hg_in, hg), (gg_in, gg)]
    for k in range(PIECES):
        at = pl.ds(k * (FB // PIECES), FB // PIECES)
        copies.append((wg_in.at[at], wg.at[at]))
    copies = [pltpu.make_async_copy(a, b, sems.at[k]) for k, (a, b) in enumerate(copies)]
    for copy in copies:
        copy.start()
    for copy in copies:
        copy.wait()


def layer(hidden_in, weights, gates, group_ids, slot_ids, out_grad):
    vmem = pl.BlockSpec(memory_space=pltpu.VMEM)
    anywhere = pl.BlockSpec(memory_space=pl.ANY)
    sem = pltpu.SemaphoreType.DMA

    def buf(*shape):
        return pltpu.VMEM(shape, BF)

    gate_row = gates.reshape(1, TOK)
    results = pl.pallas_call(
        kernel,
        out_shape=(
            pltpu.VMEM((TOK, D), BF),
            pltpu.VMEM((TOK, FF), BF),
            pltpu.VMEM((FB, D), BF),
            pltpu.VMEM((1, TOK), F32),
        ),
        in_specs=[anywhere, anywhere, vmem, vmem, vmem, anywhere],
        out_specs=(vmem, vmem, vmem, vmem),
        scratch_shapes=[
            buf(FB, D),
            buf(NZ * ROWS, FB),
            buf(MAIN, FB),
            buf(NZ * ROWS, D),
            buf(MAIN, XD),
            buf(8 * TOK, FB),
            buf(NZ * MAIN, FB),
            buf(MAIN, FB),
            buf(2 * TOK, HD),
            buf(TOK, HD),
            buf(MAIN, HD),
            buf(MAIN, XD),
            buf(NZ * ROWS, HD),
            buf(NZ * ROWS, HD),
            buf(2, ROWS, QD),
            buf(2, ROWS, HD),
            buf(NZ * ROWS, FB),
            buf(NZ * MAIN, FB),
            buf(MAIN, FB),
            buf(TOK, HD),
            buf(TOK, D),
            buf(NZ * MAIN, 2 * TOK),
            buf(NZ * MAIN, TOK),
            pltpu.VMEM((8 * 8, TOK), jnp.int32),
            sem((1,)), sem((1,)),
            sem((1,)), sem((1,)),
            sem((1,)), sem((1,)), sem((1,)),
            sem((1,)), sem((1,)),
            sem((2,)), sem((2,)),
            sem((1,)), sem((1,)),
            sem((5,)), sem((5,)),
            sem((4,)), sem((4,)),
            sem((2,)), sem((2,)),
            sem((4,)), sem((4,)),
            sem((4,)), sem((4,)),
            sem((12,)), sem((12,)),
            sem((5,)), sem((5,)),
            sem((4,)), sem((4,)),
            sem((2,)), sem((2,)),
            sem((1,)), sem((1,)),
        ],
        compiler_params=pltpu.CompilerParams(
            collective_id=0, has_side_effects=True, vmem_limit_bytes=55104 * 1024
        ),
        cost_estimate=pl.CostEstimate(
            flops=6 * NZ * ROWS * FB * D, bytes_accessed=20_000_000, transcendentals=0
        ),
        name="experts",
    )(hidden_in, weights, gate_row, group_ids.reshape(1, TOK), slot_ids.reshape(1, TOK), out_grad)

    results = [pltpu.with_memory_space_constraint(value, pltpu.VMEM) for value in results]
    mixed, hidden_grad, weight_grad, gate_grad = pl.pallas_call(
        finish,
        out_shape=(
            jax.ShapeDtypeStruct((TOK, D), BF),
            jax.ShapeDtypeStruct((TOK, FF), BF),
            jax.ShapeDtypeStruct((FB, D), BF),
            jax.ShapeDtypeStruct((1, TOK), F32),
        ),
        in_specs=[vmem, vmem, vmem, vmem],
        out_specs=(anywhere, anywhere, anywhere, anywhere),
        scratch_shapes=[sem((PIECES + 3,))],
        compiler_params=pltpu.CompilerParams(vmem_limit_bytes=40 * 1024 * 1024),
        name="finish",
    )(*results)
    return mixed, hidden_grad, weight_grad, gate_grad.reshape(TOK)


def solution(mesh):
    wide, flat = P(("grp", "exp"), None), P(("grp", "exp"))
    return jax.shard_map(
        layer,
        mesh=mesh,
        in_specs=(wide, wide, flat, flat, flat, wide),
        out_specs=(wide, wide, wide, flat),
        check_vma=False,
    )
```

```python
import functools

import jax
import jax.numpy as jnp
from jax import lax
from jax.experimental import pallas as pl
from jax.experimental.pallas import tpu as pltpu
from jax.sharding import PartitionSpec as P

MESH = pl.DeviceIdType.MESH
BF = jnp.bfloat16
F32 = jnp.float32
TOK, CAP = 128, 10
D, FF, FB = 4096, 7168, 896
HD, QD, XD = D // 2, D // 4, D // 8
NP, NZ = 16, 4
MAIN, EXT, ROWS = 256, 64, 320


def hops(k):
    return min(k, 4 - k)


PLANE = sorted(
    [(i, j) for i in range(4) for j in range(4) if i + j], key=lambda o: -(hops(o[0]) + hops(o[1]))
)
COLUMN = [(0, 2), (1, 2), (0, 1), (0, 3), (1, 1), (1, 3), (1, 0)]


def dot(a, b, dims=((1,), (0,))):
    return lax.dot_general(a, b, (dims, ((), ())), preferred_element_type=F32)


def dot_tn(a, b):
    return dot(a, b, ((0,), (0,)))


def dot_nt(a, b):
    return dot(a, b, ((1,), (1,)))


def one(cond):
    return jnp.where(cond, 1.0, 0.0).astype(F32).astype(BF)


def iota(shape, dim):
    return lax.broadcasted_iota(jnp.int32, shape, dim)


def mult(value, of):
    return pl.multiple_of(value, of)


def kernel(
    hid, w_hbm, gates, group_ids, slot_ids, og_hbm,
    mixed, hg, wg, gg,
    wv, h, hxr, cot, cxp, xh, sm, sx, tok, tsend, gm, gx, pa, prcv, r1, r2, hp, rm, rx, kr, og,
    mt, xb, posv,
    pos_s, pos_r, hz_s, hz_r, w_sem, og_sem, st_sem, t_s, t_r, cm_s, cm_r, cx_s, cx_r, hm_s, hm_r,
    ag_s, ag_r, agf_s, agf_r, sib_s, sib_r, po_s, po_r, rs_s, rs_r, ret_s, ret_r, eo_s, eo_r, k_s, k_r, hg_s, hg_r,
):
    g = lax.axis_index("grp")
    z = lax.axis_index("exp")
    c = lax.rem(g, 2)
    p = lax.div(g, 2)
    x = lax.div(p, 4)
    y = lax.rem(p, 4)
    nc = 1 - c
    zp = lax.rem(z + 1, 4)
    zm = lax.rem(z + 3, 4)
    zo = lax.rem(z + 2, 4)
    sib = (p * 2 + nc, z)
    up = (g, zp)
    down = (g, zm)
    blk = c * 4 + z
    kk, hpx, ex, em, exr = prcv, sx, gx, tok, cxp

    def plane(i, j):
        p2 = lax.rem(x + i, 4) * 4 + lax.rem(y + j, 4)
        return p2, (p2 * 2 + c, z)

    def column(dc, dz):
        c2 = lax.rem(c + dc, 2)
        z2 = lax.rem(z + dz, 4)
        return c2, z2, (p * 2 + c2, z2)

    def remote(src, dst, ss, rs, dev):
        return pltpu.make_async_remote_copy(
            src_ref=src, dst_ref=dst, send_sem=ss, recv_sem=rs, device_id=dev, device_id_type=MESH
        )

    def local(src, dst, sem):
        return pltpu.make_async_copy(src, dst, sem)

    def drain(ref, sem):
        pltpu.make_async_copy(ref, ref, sem).wait()

    def rows(ref, start, size, of=16):
        return ref.at[pl.ds(mult(start, of), size)]

    def cols(start, size):
        return pl.ds(mult(start, 128), size)

    barrier = pltpu.get_barrier_semaphore()
    for dc, dz in COLUMN:
        pl.semaphore_signal(barrier, inc=1, device_id=column(dc, dz)[2], device_id_type=MESH)
    for i, j in PLANE:
        pl.semaphore_signal(barrier, inc=1, device_id=plane(i, j)[1], device_id_type=MESH)

    local(og_hbm, og, og_sem.at[0]).start()
    for k in range(8):
        local(hid.at[:, pl.ds(k * FB, FB)], hp.at[pl.ds(k * TOK, TOK)], st_sem.at[0]).start()
    local(w_hbm, wv, w_sem.at[0]).start()
    position = group_ids[...] * CAP + slot_ids[...]
    posv[pl.ds(mult((z * 2 + c) * 8, 8), 8), :] = jnp.broadcast_to(position, (8, TOK))
    eye = iota((TOK, TOK), 0) == iota((TOK, TOK), 1)
    gate = jnp.sum(jnp.where(eye, gates[...], 0.0), axis=1, keepdims=True)
    drain(og, og_sem.at[0])
    tsend[...] = (gate * og[:, cols(nc * HD, HD)].astype(F32)).astype(BF)
    drain(hp.at[pl.ds(0, 8 * TOK)], st_sem.at[0])
    pl.semaphore_wait(barrier, len(COLUMN) + len(PLANE))

    remote(tsend, rows(tok, c * TOK, TOK), t_s.at[0], t_r.at[0], sib).start()
    mine = rows(posv, (z * 2 + c) * 8, 8, 8)
    for dc, dz in COLUMN:
        remote(mine, mine, pos_s.at[0], pos_r.at[0], column(dc, dz)[2]).start()

    def send_hidden(piece, _):
        for dc, dz in COLUMN:
            c2, z2, dev = column(dc, dz)
            src = rows(hp, (c2 * 4 + z2) * TOK + piece * 32, 32)
            dst = rows(xh, (z * 2 + c) * TOK + piece * 32, 32)
            remote(src, dst, hz_s.at[0], hz_r.at[0], dev).start()
        return 0

    lax.fori_loop(0, 4, send_hidden, 0)
    local(rows(hp, blk * TOK, TOK), rows(xh, (z * 2 + c) * TOK, TOK), hz_r.at[0]).start()
    tok[pl.ds(mult(c * TOK, 16), TOK), :] = (gate * og[:, cols(c * HD, HD)].astype(F32)).astype(BF)

    drain(rows(posv, 0, 56, 8), pos_r.at[0])

    def tables(zz, _):
        group = iota((MAIN, TOK), 0) // 16
        slot = iota((MAIN, TOK), 0) % 16
        both = posv[pl.ds(mult(zz * 16, 16), 16), :]
        first, second = both[0:1, :], both[8:9, :]
        at = pl.ds(mult(zz * MAIN, 16), MAIN)
        mt[at, 0:TOK] = one((slot < CAP) & (group * CAP + slot == first))
        mt[at, TOK : 2 * TOK] = one((slot >= CAP) & (group * CAP + slot - CAP == second))
        xb[at, :] = one(group * CAP + slot % 4 + 6 == second)
        return 0

    lax.fori_loop(0, NZ, tables, 0)
    part = (iota((MAIN, TOK), 0) // 4) % 4

    def extra_pick(zz, q):
        base = xb[pl.ds(mult(zz * MAIN, 16), MAIN), :]
        return jnp.where(part == q, base.astype(F32), 0.0).astype(BF)

    def table(zz):
        return mt[pl.ds(mult(zz * MAIN, 16), MAIN), :]

    def half(ref, start, size, n):
        return ref.at[pl.ds(mult(start, 16), size), pl.ds(n * QD, QD)]

    def cot_half(start, size, n):
        return cot.at[pl.ds(mult(start, 16), size), cols(c * HD + n * QD, QD)]

    def send_slots(src, dst, ss, rs):
        for i, j in PLANE:
            p2, dev = plane(i, j)
            remote(src(p2), dst, ss, rs, dev).start()
        local(src(p), dst, rs).start()

    drain(tsend, t_r.at[0])
    gx[...] = sum(
        dot(extra_pick(z, q), tok[TOK : 2 * TOK, q * XD : (q + 1) * XD]) for q in range(4)
    ).astype(BF)
    send_slots(lambda p2: rows(gx, p2 * 16, 16), rows(cxp, p * 16, 16), cx_s.at[0], cx_r.at[0])
    for n in range(2):
        gm[:, n * QD : (n + 1) * QD] = dot(table(z), tok[:, n * QD : (n + 1) * QD]).astype(BF)
        send_slots(
            lambda p2: half(gm, p2 * 16, 16, n), cot_half(z * ROWS + p * 16, 16, n), cm_s.at[n], cm_r.at[n]
        )

    def cot_block(zz, start, size):
        return cot.at[pl.ds(mult(zz * ROWS, 16), ROWS), cols(c * HD + start, size)]

    def to_sibling(zz):
        ref = cot_block(zz, 0, HD)
        remote(ref, ref, sib_s.at[zz], sib_r.at[zz], sib).start()

    drain(cxp, cx_r.at[0])
    place = (iota((EXT, MAIN), 0) // 4 == iota((EXT, MAIN), 1) // 16) & (
        iota((EXT, MAIN), 0) % 4 == iota((EXT, MAIN), 1) % 4
    )
    for q in range(4):
        unpack = one(place & ((iota((EXT, MAIN), 1) // 4) % 4 == q))
        cot[pl.ds(mult(z * ROWS + MAIN, 16), EXT), cols(c * HD + q * XD, XD)] = dot(
            unpack, cxp[...]
        ).astype(BF)
    for n in range(2):
        drain(cot_half(z * ROWS, MAIN, n), cm_r.at[n])
        ref = cot_block(z, n * QD, QD)
        remote(ref, ref, ag_s.at[2 * n], ag_r.at[2 * n], up).start()
        remote(ref, ref, ag_s.at[2 * n + 1], ag_r.at[2 * n + 1], down).start()
    to_sibling(z)

    drain(xh, hz_r.at[0])
    sx[...] = sum(
        dot(extra_pick(zz, zz), xh[(2 * zz + 1) * TOK : (2 * zz + 2) * TOK, :]) for zz in range(NZ)
    ).astype(BF)

    send_slots(lambda p2: rows(sx, p2 * 16, 16), rows(hxr, p * 16, 16), hm_s.at[4], hm_r.at[4])

    def order(k):
        return lax.rem(z + jnp.where(k == 2, 3, jnp.where(k == 3, 0, 2 - k)), 4)

    def pick_hidden(k, _):
        zz = order(k)
        at = pl.ds(mult(zz * MAIN, 16), MAIN)
        sm[at, :] = dot(table(zz), xh[at, :]).astype(BF)
        send_slots(
            lambda p2: rows(sm, zz * MAIN + p2 * 16, 16),
            rows(h, zz * ROWS + p * 16, 16),
            hm_s.at[zz],
            hm_r.at[zz],
        )
        return 0

    lax.fori_loop(0, NZ, pick_hidden, 0)

    drain(wv, w_sem.at[0])

    drain(hp.at[pl.ds(0, 7 * TOK)], hz_s.at[0])

    def slot_grads(zz):
        at = pl.ds(mult(zz * ROWS, 16), ROWS)
        hp[at, :] = dot_nt(cot[at, :], wv[...]).astype(BF)
        send_slots(
            lambda p2: rows(hp, zz * ROWS + p2 * 16, 16),
            rows(rm, zz * MAIN + p * 16, 16),
            ret_s.at[zz],
            ret_r.at[zz],
        )

    def other_half(zz):
        return cot.at[pl.ds(mult(zz * ROWS, 16), ROWS), cols(nc * HD, HD)]

    drain(other_half(z), sib_r.at[z])
    slot_grads(z)

    mine_out = pa

    def other_out(zz):
        return wg.at[pl.ds(mult(lax.div(zz, 2) * ROWS, 16), ROWS), cols(lax.rem(zz, 2) * HD, HD)]

    drain(hxr, hm_r.at[4])
    swap = one(
        (iota((MAIN, MAIN), 0) // 64 == (iota((MAIN, MAIN), 1) // 4) % 4)
        & ((iota((MAIN, MAIN), 0) // 4) % 16 == iota((MAIN, MAIN), 1) // 16)
        & (iota((MAIN, MAIN), 0) % 4 == iota((MAIN, MAIN), 1) % 4)
    )
    moved = dot(swap, hxr[...]).astype(BF)
    for zz in range(NZ):
        h[zz * ROWS + MAIN : (zz + 1) * ROWS, :] = moved[zz * EXT : (zz + 1) * EXT, :]

    def add_into(zz, start, size, ref):
        def step(i, _):
            at = pl.ds(mult(zz * ROWS + i * 32, 16), 32)
            where = cols(start, size)
            mine_out[at, where] = (
                mine_out[at, where].astype(F32) + ref(i)[...].astype(F32)
            ).astype(BF)
            return 0

        lax.fori_loop(0, ROWS // 32, step, 0)

    def add_cores(zz):
        drain(prcv.at[pl.ds(mult(zz * ROWS, 16), ROWS)], po_r.at[zz])
        add_into(zz, 0, HD, lambda i: prcv.at[pl.ds(mult(zz * ROWS + i * 32, 16), 32)])

    def sum_block(zz, n, s):
        return mine_out.at[pl.ds(mult(zz * ROWS, 16), ROWS), pl.ds(n * QD + s * XD, XD)]

    def r1_block(n, s):
        return r1.at[n, :, pl.ds(s * XD, XD)]

    def r2_block(side, n, s):
        return r2.at[side, :, pl.ds(n * QD + s * XD, XD)]

    def send_sum(src, dst, kind, s, dev):
        remote(src, dst, rs_s.at[2 * kind + s], rs_r.at[2 * kind + s], dev).start()

    def partials(k, _):
        zz = order(k)
        at = pl.ds(mult(zz * ROWS, 16), ROWS)

        @pl.when(k == 0)
        def _():
            drain(cot_block(zm, 0, QD), ag_r.at[0])
            ref = cot_block(zm, 0, QD)
            remote(ref, ref, agf_s.at[0], agf_r.at[0], up).start()
            drain(cot_block(zp, QD, QD), ag_r.at[3])
            ref2 = cot_block(zp, QD, QD)
            remote(ref2, ref2, agf_s.at[1], agf_r.at[1], down).start()

        drain(h.at[pl.ds(mult(zz * ROWS, 16), MAIN)], hm_r.at[zz])
        rows_in = h[at, :]

        def product(out, part):
            def tile(j, _):
                out[:, cols(j * QD, QD)] = dot(
                    rows_in, wv[:, cols(part * HD + j * QD, QD)]
                ).astype(BF)
                return 0

            lax.fori_loop(0, 2, tile, 0)

        product(other_out(zz), nc)
        remote(other_out(zz), prcv.at[at], po_s.at[zz], po_r.at[zz], sib).start()
        product(mine_out.at[at], c)

        @pl.when(k == 1)
        def _():
            add_cores(zo)
            for s in range(2):
                send_sum(sum_block(zo, 0, s), r1_block(0, s), 0, s, up)
                send_sum(sum_block(zo, 1, s), r1_block(1, s), 1, s, down)

        @pl.when(k == 2)
        def _():
            add_cores(zp)
            for s in range(2):
                send_sum(sum_block(zp, 1, s), r2_block(0, 1, s), 2, s, up)
            drain(cot_block(zm, QD, QD), ag_r.at[2])
            to_sibling(zm)
            drain(cot_block(zp, 0, QD), ag_r.at[1])
            to_sibling(zp)

        @pl.when(k == 3)
        def _():
            add_cores(zm)
            for s in range(2):
                send_sum(sum_block(zm, 0, s), r2_block(1, 0, s), 3, s, down)

        return 0

    lax.fori_loop(0, NZ, partials, 0)
    add_cores(z)

    def more_grads(k, _):
        zz = lax.rem(z + jnp.where(k == 0, 1, jnp.where(k == 1, 3, 2)), 4)

        @pl.when(k == 2)
        def _():
            drain(cot_block(zo, 0, QD), agf_r.at[0])
            drain(cot_block(zo, QD, QD), agf_r.at[1])
            to_sibling(zo)

        drain(other_half(zz), sib_r.at[zz])
        slot_grads(zz)
        return 0

    lax.fori_loop(0, 2, more_grads, 0)

    for s in range(2):
        for n, zz, dev in ((0, zp, up), (1, zm, down)):
            drain(r1_block(n, s), rs_r.at[2 * n + s])
            add_into(
                zz,
                n * QD + s * XD,
                XD,
                lambda i: r1.at[n, pl.ds(mult(i * 32, 16), 32), pl.ds(s * XD, XD)],
            )
            send_sum(sum_block(zz, n, s), r2_block(n, n, s), 4 + n, s, dev)

    more_grads(jnp.int32(2), 0)

    unswap = one(
        (iota((MAIN, MAIN), 1) // 64 == (iota((MAIN, MAIN), 0) // 4) % 4)
        & ((iota((MAIN, MAIN), 1) // 4) % 16 == iota((MAIN, MAIN), 0) // 16)
        & (iota((MAIN, MAIN), 1) % 4 == iota((MAIN, MAIN), 0) % 4)
    )
    drain(hp.at[pl.ds(0, 240)], hm_s.at[4])
    hpx[...] = sum(
        dot(unswap[:, zz * EXT : (zz + 1) * EXT], hp[zz * ROWS + MAIN : (zz + 1) * ROWS, :])
        for zz in range(NZ)
    ).astype(BF)
    send_slots(lambda p2: rows(hpx, p2 * 16, 16), rows(rx, p * 16, 16), ret_s.at[4], ret_r.at[4])

    for zz in range(NZ):
        drain(prcv.at[0:ROWS], po_s.at[zz])

    def weight_grads(j, _):
        at = cols(j * XD, XD)
        wg[:, at] = dot_tn(h[...], cot[:, at]).astype(BF)
        return 0

    lax.fori_loop(0, 8, weight_grads, 0)

    drain(rx, ret_r.at[4])

    def tokens_grad(zz, _):
        at = pl.ds(mult(zz * MAIN, 16), MAIN)
        drain(rm.at[at], ret_r.at[zz])
        grads = dot_tn(table(zz), rm[at, :])
        late = dot_tn(extra_pick(zz, zz), rx[...])
        xh[pl.ds(mult(zz * MAIN, 16), TOK), :] = grads[0:TOK, :].astype(BF)
        xh[pl.ds(mult(zz * MAIN + TOK, 16), TOK), :] = (grads[TOK:, :] + late).astype(BF)
        return 0

    lax.fori_loop(0, NZ, tokens_grad, 0)

    for n in range(2):
        drain(half(gm, 0, 240, n), cm_s.at[n])
    drain(gx.at[pl.ds(0, 240)], cx_s.at[0])

    def return_grads(piece):
        for dc, dz in COLUMN:
            c2, z2, dev = column(dc, dz)
            src = rows(xh, (z2 * 2 + c2) * TOK + piece * 32, 32)
            dst = hg.at[pl.ds(mult(piece * 32, 16), 32), cols(blk * FB, FB)]
            remote(src, dst, hg_s.at[0], hg_r.at[0], dev).start()

    def last_sum(first, count, n, s):
        at = pl.ds(mult(z * ROWS + first, 16), count)
        there = pl.ds(mult(first, 16), count)
        where = pl.ds(n * QD + s * XD, XD)
        return (
            mine_out[at, where].astype(F32)
            + r2[0, there, where].astype(F32)
            + r2[1, there, where].astype(F32)
        ).astype(BF)

    back = (iota((MAIN, EXT), 1) // 4 == iota((MAIN, EXT), 0) // 16) & (
        iota((MAIN, EXT), 1) % 4 == iota((MAIN, EXT), 0) % 4
    )
    SD = XD // 2
    for s in range(2):
        for kind, side, n in ((2, 0, 1), (3, 1, 0), (4, 0, 0), (5, 1, 1)):
            drain(r2_block(side, n, s), rs_r.at[2 * kind + s])
        lax.fori_loop(2 * s, 2 + 2 * s, lambda piece, _: return_grads(piece) or 0, 0)
        for n in range(2):

            def main_rows(i, _):
                at = pl.ds(mult(i * 32, 16), 32)
                gm[at, (2 * s + n) * XD : (2 * s + n + 1) * XD] = last_sum(i * 32, 32, n, s)
                return 0

            lax.fori_loop(0, MAIN // 32, main_rows, 0)
        send_slots(
            lambda p2: half(gm, p2 * 16, 16, s), half(em, p * 16, 16, s), eo_s.at[s], eo_r.at[s]
        )
        tails = [last_sum(MAIN, EXT, n, s) for n in range(2)]
        ex[:, s * SD : (s + 1) * SD] = sum(
            dot(
                one(back & ((iota((MAIN, EXT), 0) // 4) % 4 == q)),
                tails[q // 2][:, (q % 2) * SD : (q % 2 + 1) * SD],
            )
            for q in range(4)
        ).astype(BF)
        send_slots(
            lambda p2: ex.at[pl.ds(mult(p2 * 16, 16), 16), pl.ds(s * SD, SD)],
            exr.at[pl.ds(mult(p * 16, 16), 16), pl.ds(s * SD, SD)],
            eo_s.at[2 + s],
            eo_r.at[2 + s],
        )
    local(rows(xh, (z * 2 + c) * TOK, TOK), hg.at[:, cols(blk * FB, FB)], hg_r.at[0]).start()

    for s in range(2):
        drain(half(em, 0, MAIN, s), eo_r.at[s])
        drain(exr.at[:, pl.ds(s * SD, SD)], eo_r.at[2 + s])
        rows_out = dot_tn(table(z), em[:, s * QD : (s + 1) * QD])
        late = jnp.concatenate(
            [dot_tn(extra_pick(z, q), exr[:, s * SD : (s + 1) * SD]) for q in range(4)], axis=1
        )
        kk[0:TOK, s * QD : (s + 1) * QD] = rows_out[0:TOK, :].astype(BF)
        kk[TOK : 2 * TOK, s * QD : (s + 1) * QD] = (rows_out[TOK:, :] + late).astype(BF)
        src = kk.at[pl.ds(mult(nc * TOK, 16), TOK), pl.ds(s * QD, QD)]
        remote(src, kr.at[:, pl.ds(s * QD, QD)], k_s.at[s], k_r.at[s], sib).start()

    total = jnp.zeros((TOK, 1), F32)
    for core, ref, first in ((c, kk, mult(c * TOK, 16)), (nc, kr, 0)):
        for s in range(2):
            if ref is kr:
                drain(kr.at[:, pl.ds(s * QD, QD)], k_r.at[s])
            for n in range(2):
                at = cols(core * HD + n * QD + s * XD, XD)
                picked = ref[pl.ds(first, TOK), (2 * s + n) * XD : (2 * s + n + 1) * XD].astype(F32)
                total += jnp.sum(og[:, at].astype(F32) * picked, axis=1, keepdims=True)
                mixed[:, at] = (gate * picked).astype(BF)
    gg[...] = jnp.sum(jnp.where(eye, total, 0.0), axis=0, keepdims=True)

    for s in range(2):
        drain(kr.at[:, pl.ds(s * QD, QD)], k_s.at[s])
    drain(hg, hg_r.at[0])
    drain(rows(posv, 0, 56, 8), pos_s.at[0])
    drain(xh.at[pl.ds(0, 7 * TOK)], hg_s.at[0])
    drain(tsend, t_s.at[0])
    for s in range(2):
        drain(half(em, 0, 240, s), eo_s.at[s])
        drain(exr.at[pl.ds(0, 240), pl.ds(s * SD, SD)], eo_s.at[2 + s])
    for n in range(5):
        if n < 4:
            drain(hp.at[pl.ds(0, 240)], hm_s.at[n])
        drain(hp.at[pl.ds(0, 240)], ret_s.at[n])
    for n in range(4):
        drain(r1.at[0], ag_s.at[n])
        drain(r2.at[0], sib_s.at[n])
    for n in range(2):
        drain(r1.at[0], agf_s.at[n])
    for n in range(12):
        drain(r1_block(0, 0), rs_s.at[n])


PIECES = 4


def finish(mixed_in, hg_in, wg_in, gg_in, mixed, hg, wg, gg, sems):
    copies = [(mixed_in, mixed), (hg_in, hg), (gg_in, gg)]
    for k in range(PIECES):
        at = pl.ds(k * (FB // PIECES), FB // PIECES)
        copies.append((wg_in.at[at], wg.at[at]))
    copies = [pltpu.make_async_copy(a, b, sems.at[k]) for k, (a, b) in enumerate(copies)]
    for copy in copies:
        copy.start()
    for copy in copies:
        copy.wait()


def layer(hidden_in, weights, gates, group_ids, slot_ids, out_grad):
    vmem = pl.BlockSpec(memory_space=pltpu.VMEM)
    anywhere = pl.BlockSpec(memory_space=pl.ANY)
    sem = pltpu.SemaphoreType.DMA

    def buf(*shape):
        return pltpu.VMEM(shape, BF)

    gate_row = gates.reshape(1, TOK)
    results = pl.pallas_call(
        kernel,
        out_shape=(
            pltpu.VMEM((TOK, D), BF),
            pltpu.VMEM((TOK, FF), BF),
            pltpu.VMEM((FB, D), BF),
            pltpu.VMEM((1, TOK), F32),
        ),
        in_specs=[anywhere, anywhere, vmem, vmem, vmem, anywhere],
        out_specs=(vmem, vmem, vmem, vmem),
        scratch_shapes=[
            buf(FB, D),
            buf(NZ * ROWS, FB),
            buf(MAIN, FB),
            buf(NZ * ROWS, D),
            buf(MAIN, XD),
            buf(8 * TOK, FB),
            buf(NZ * MAIN, FB),
            buf(MAIN, FB),
            buf(2 * TOK, HD),
            buf(TOK, HD),
            buf(MAIN, HD),
            buf(MAIN, XD),
            buf(NZ * ROWS, HD),
            buf(NZ * ROWS, HD),
            buf(2, ROWS, QD),
            buf(2, ROWS, HD),
            buf(NZ * ROWS, FB),
            buf(NZ * MAIN, FB),
            buf(MAIN, FB),
            buf(TOK, HD),
            buf(TOK, D),
            buf(NZ * MAIN, 2 * TOK),
            buf(NZ * MAIN, TOK),
            pltpu.VMEM((8 * 8, TOK), jnp.int32),
            sem((1,)), sem((1,)),
            sem((1,)), sem((1,)),
            sem((1,)), sem((1,)), sem((1,)),
            sem((1,)), sem((1,)),
            sem((2,)), sem((2,)),
            sem((1,)), sem((1,)),
            sem((5,)), sem((5,)),
            sem((4,)), sem((4,)),
            sem((2,)), sem((2,)),
            sem((4,)), sem((4,)),
            sem((4,)), sem((4,)),
            sem((12,)), sem((12,)),
            sem((5,)), sem((5,)),
            sem((4,)), sem((4,)),
            sem((2,)), sem((2,)),
            sem((1,)), sem((1,)),
        ],
        compiler_params=pltpu.CompilerParams(
            collective_id=0, has_side_effects=True, vmem_limit_bytes=55104 * 1024
        ),
        cost_estimate=pl.CostEstimate(
            flops=6 * NZ * ROWS * FB * D, bytes_accessed=20_000_000, transcendentals=0
        ),
        name="experts",
    )(hidden_in, weights, gate_row, group_ids.reshape(1, TOK), slot_ids.reshape(1, TOK), out_grad)

    results = [pltpu.with_memory_space_constraint(value, pltpu.VMEM) for value in results]
    mixed, hidden_grad, weight_grad, gate_grad = pl.pallas_call(
        finish,
        out_shape=(
            jax.ShapeDtypeStruct((TOK, D), BF),
            jax.ShapeDtypeStruct((TOK, FF), BF),
            jax.ShapeDtypeStruct((FB, D), BF),
            jax.ShapeDtypeStruct((1, TOK), F32),
        ),
        in_specs=[vmem, vmem, vmem, vmem],
        out_specs=(anywhere, anywhere, anywhere, anywhere),
        scratch_shapes=[sem((PIECES + 3,))],
        compiler_params=pltpu.CompilerParams(vmem_limit_bytes=40 * 1024 * 1024),
        name="finish",
    )(*results)
    return mixed, hidden_grad, weight_grad, gate_grad.reshape(TOK)


def solution(mesh):
    wide, flat = P(("grp", "exp"), None), P(("grp", "exp"))
    return jax.shard_map(
        layer,
        mesh=mesh,
        in_specs=(wide, wide, flat, flat, flat, wide),
        out_specs=(wide, wide, wide, flat),
        check_vma=False,
    )
```

```python
import functools

import jax
import jax.numpy as jnp
from jax import lax
from jax.experimental import pallas as pl
from jax.experimental.pallas import tpu as pltpu
from jax.sharding import PartitionSpec as P

MESH = pl.DeviceIdType.MESH
BF = jnp.bfloat16
F32 = jnp.float32
TOK, CAP = 128, 10
D, FF, FB = 4096, 7168, 896
HD, QD, XD = D // 2, D // 4, D // 8
NP, NZ = 16, 4
MAIN, EXT, ROWS = 256, 64, 320


def hops(k):
    return min(k, 4 - k)


PLANE = sorted(
    [(i, j) for i in range(4) for j in range(4) if i + j], key=lambda o: -(hops(o[0]) + hops(o[1]))
)
COLUMN = [(0, 2), (1, 2), (0, 1), (0, 3), (1, 1), (1, 3), (1, 0)]


def dot(a, b, dims=((1,), (0,))):
    return lax.dot_general(a, b, (dims, ((), ())), preferred_element_type=F32)


def dot_tn(a, b):
    return dot(a, b, ((0,), (0,)))


def dot_nt(a, b):
    return dot(a, b, ((1,), (1,)))


def one(cond):
    return jnp.where(cond, 1.0, 0.0).astype(F32).astype(BF)


def iota(shape, dim):
    return lax.broadcasted_iota(jnp.int32, shape, dim)


def mult(value, of):
    return pl.multiple_of(value, of)


def kernel(
    hid, w_hbm, gates, group_ids, slot_ids, og_hbm,
    mixed, hg, wg, gg,
    wv, h, hxr, cot, cxp, xh, sm, sx, tok, tsend, gm, gx, pa, prcv, r1, r2, hp, rm, rx, kr, og,
    mt, xb, posv,
    pos_s, pos_r, hz_s, hz_r, w_sem, og_sem, st_sem, t_s, t_r, cm_s, cm_r, cx_s, cx_r, hm_s, hm_r,
    ag_s, ag_r, agf_s, agf_r, sib_s, sib_r, po_s, po_r, rs_s, rs_r, ret_s, ret_r, eo_s, eo_r, k_s, k_r, hg_s, hg_r,
):
    g = lax.axis_index("grp")
    z = lax.axis_index("exp")
    c = lax.rem(g, 2)
    p = lax.div(g, 2)
    x = lax.div(p, 4)
    y = lax.rem(p, 4)
    nc = 1 - c
    zp = lax.rem(z + 1, 4)
    zm = lax.rem(z + 3, 4)
    zo = lax.rem(z + 2, 4)
    sib = (p * 2 + nc, z)
    up = (g, zp)
    down = (g, zm)
    blk = c * 4 + z
    kk, hpx, ex, em, exr = prcv, sx, gx, tok, cxp

    def plane(i, j):
        p2 = lax.rem(x + i, 4) * 4 + lax.rem(y + j, 4)
        return p2, (p2 * 2 + c, z)

    def column(dc, dz):
        c2 = lax.rem(c + dc, 2)
        z2 = lax.rem(z + dz, 4)
        return c2, z2, (p * 2 + c2, z2)

    def remote(src, dst, ss, rs, dev):
        return pltpu.make_async_remote_copy(
            src_ref=src, dst_ref=dst, send_sem=ss, recv_sem=rs, device_id=dev, device_id_type=MESH
        )

    def local(src, dst, sem):
        return pltpu.make_async_copy(src, dst, sem)

    def drain(ref, sem):
        pltpu.make_async_copy(ref, ref, sem).wait()

    def rows(ref, start, size, of=16):
        return ref.at[pl.ds(mult(start, of), size)]

    def cols(start, size):
        return pl.ds(mult(start, 128), size)

    barrier = pltpu.get_barrier_semaphore()
    for dc, dz in COLUMN:
        pl.semaphore_signal(barrier, inc=1, device_id=column(dc, dz)[2], device_id_type=MESH)
    for i, j in PLANE:
        pl.semaphore_signal(barrier, inc=1, device_id=plane(i, j)[1], device_id_type=MESH)

    local(og_hbm, og, og_sem.at[0]).start()
    for k in range(8):
        local(hid.at[:, pl.ds(k * FB, FB)], hp.at[pl.ds(k * TOK, TOK)], st_sem.at[0]).start()
    local(w_hbm, wv, w_sem.at[0]).start()
    position = group_ids[...] * CAP + slot_ids[...]
    posv[pl.ds(mult((z * 2 + c) * 8, 8), 8), :] = jnp.broadcast_to(position, (8, TOK))
    eye = iota((TOK, TOK), 0) == iota((TOK, TOK), 1)
    gate = jnp.sum(jnp.where(eye, gates[...], 0.0), axis=1, keepdims=True)
    drain(og, og_sem.at[0])
    tsend[...] = (gate * og[:, cols(nc * HD, HD)].astype(F32)).astype(BF)
    drain(hp.at[pl.ds(0, 8 * TOK)], st_sem.at[0])
    pl.semaphore_wait(barrier, len(COLUMN) + len(PLANE))

    remote(tsend, rows(tok, c * TOK, TOK), t_s.at[0], t_r.at[0], sib).start()
    mine = rows(posv, (z * 2 + c) * 8, 8, 8)
    for dc, dz in COLUMN:
        remote(mine, mine, pos_s.at[0], pos_r.at[0], column(dc, dz)[2]).start()

    def send_hidden(piece, _):
        for dc, dz in COLUMN:
            c2, z2, dev = column(dc, dz)
            src = rows(hp, (c2 * 4 + z2) * TOK + piece * 32, 32)
            dst = rows(xh, (z * 2 + c) * TOK + piece * 32, 32)
            remote(src, dst, hz_s.at[0], hz_r.at[0], dev).start()
        return 0

    lax.fori_loop(0, 4, send_hidden, 0)
    local(rows(hp, blk * TOK, TOK), rows(xh, (z * 2 + c) * TOK, TOK), hz_r.at[0]).start()
    tok[pl.ds(mult(c * TOK, 16), TOK), :] = (gate * og[:, cols(c * HD, HD)].astype(F32)).astype(BF)

    drain(rows(posv, 0, 56, 8), pos_r.at[0])

    def tables(zz, _):
        group = iota((MAIN, TOK), 0) // 16
        slot = iota((MAIN, TOK), 0) % 16
        both = posv[pl.ds(mult(zz * 16, 16), 16), :]
        first, second = both[0:1, :], both[8:9, :]
        at = pl.ds(mult(zz * MAIN, 16), MAIN)
        mt[at, 0:TOK] = one((slot < CAP) & (group * CAP + slot == first))
        mt[at, TOK : 2 * TOK] = one((slot >= CAP) & (group * CAP + slot - CAP == second))
        xb[at, :] = one(group * CAP + slot % 4 + 6 == second)
        return 0

    lax.fori_loop(0, NZ, tables, 0)
    part = (iota((MAIN, TOK), 0) // 4) % 4

    def extra_pick(zz, q):
        base = xb[pl.ds(mult(zz * MAIN, 16), MAIN), :]
        return jnp.where(part == q, base.astype(F32), 0.0).astype(BF)

    def table(zz):
        return mt[pl.ds(mult(zz * MAIN, 16), MAIN), :]

    def half(ref, start, size, n):
        return ref.at[pl.ds(mult(start, 16), size), pl.ds(n * QD, QD)]

    def cot_half(start, size, n):
        return cot.at[pl.ds(mult(start, 16), size), cols(c * HD + n * QD, QD)]

    def send_slots(src, dst, ss, rs):
        for i, j in PLANE:
            p2, dev = plane(i, j)
            remote(src(p2), dst, ss, rs, dev).start()
        local(src(p), dst, rs).start()

    drain(tsend, t_r.at[0])
    gx[...] = sum(
        dot(extra_pick(z, q), tok[TOK : 2 * TOK, q * XD : (q + 1) * XD]) for q in range(4)
    ).astype(BF)
    send_slots(lambda p2: rows(gx, p2 * 16, 16), rows(cxp, p * 16, 16), cx_s.at[0], cx_r.at[0])
    for n in range(2):
        gm[:, n * QD : (n + 1) * QD] = dot(table(z), tok[:, n * QD : (n + 1) * QD]).astype(BF)
        send_slots(
            lambda p2: half(gm, p2 * 16, 16, n), cot_half(z * ROWS + p * 16, 16, n), cm_s.at[n], cm_r.at[n]
        )

    def cot_block(zz, start, size):
        return cot.at[pl.ds(mult(zz * ROWS, 16), ROWS), cols(c * HD + start, size)]

    def to_sibling(zz):
        ref = cot_block(zz, 0, HD)
        remote(ref, ref, sib_s.at[zz], sib_r.at[zz], sib).start()

    drain(cxp, cx_r.at[0])
    place = (iota((EXT, MAIN), 0) // 4 == iota((EXT, MAIN), 1) // 16) & (
        iota((EXT, MAIN), 0) % 4 == iota((EXT, MAIN), 1) % 4
    )
    for q in range(4):
        unpack = one(place & ((iota((EXT, MAIN), 1) // 4) % 4 == q))
        cot[pl.ds(mult(z * ROWS + MAIN, 16), EXT), cols(c * HD + q * XD, XD)] = dot(
            unpack, cxp[...]
        ).astype(BF)
    for n in range(2):
        drain(cot_half(z * ROWS, MAIN, n), cm_r.at[n])
        ref = cot_block(z, n * QD, QD)
        remote(ref, ref, ag_s.at[2 * n], ag_r.at[2 * n], up).start()
        remote(ref, ref, ag_s.at[2 * n + 1], ag_r.at[2 * n + 1], down).start()
    to_sibling(z)

    drain(xh, hz_r.at[0])
    sx[...] = sum(
        dot(extra_pick(zz, zz), xh[(2 * zz + 1) * TOK : (2 * zz + 2) * TOK, :]) for zz in range(NZ)
    ).astype(BF)

    send_slots(lambda p2: rows(sx, p2 * 16, 16), rows(hxr, p * 16, 16), hm_s.at[4], hm_r.at[4])

    def order(k):
        return lax.rem(z + jnp.where(k == 2, 3, jnp.where(k == 3, 0, 2 - k)), 4)

    def pick_hidden(k, _):
        zz = order(k)
        at = pl.ds(mult(zz * MAIN, 16), MAIN)
        sm[at, :] = dot(table(zz), xh[at, :]).astype(BF)
        send_slots(
            lambda p2: rows(sm, zz * MAIN + p2 * 16, 16),
            rows(h, zz * ROWS + p * 16, 16),
            hm_s.at[zz],
            hm_r.at[zz],
        )
        return 0

    lax.fori_loop(0, NZ, pick_hidden, 0)

    drain(wv, w_sem.at[0])

    drain(hp.at[pl.ds(0, 7 * TOK)], hz_s.at[0])

    def slot_grads(zz):
        at = pl.ds(mult(zz * ROWS, 16), ROWS)
        hp[at, :] = dot_nt(cot[at, :], wv[...]).astype(BF)
        send_slots(
            lambda p2: rows(hp, zz * ROWS + p2 * 16, 16),
            rows(rm, zz * MAIN + p * 16, 16),
            ret_s.at[zz],
            ret_r.at[zz],
        )

    def other_half(zz):
        return cot.at[pl.ds(mult(zz * ROWS, 16), ROWS), cols(nc * HD, HD)]

    drain(other_half(z), sib_r.at[z])
    slot_grads(z)

    mine_out = pa

    def other_out(zz):
        return wg.at[pl.ds(mult(lax.div(zz, 2) * ROWS, 16), ROWS), cols(lax.rem(zz, 2) * HD, HD)]

    drain(hxr, hm_r.at[4])
    swap = one(
        (iota((MAIN, MAIN), 0) // 64 == (iota((MAIN, MAIN), 1) // 4) % 4)
        & ((iota((MAIN, MAIN), 0) // 4) % 16 == iota((MAIN, MAIN), 1) // 16)
        & (iota((MAIN, MAIN), 0) % 4 == iota((MAIN, MAIN), 1) % 4)
    )
    moved = dot(swap, hxr[...]).astype(BF)
    for zz in range(NZ):
        h[zz * ROWS + MAIN : (zz + 1) * ROWS, :] = moved[zz * EXT : (zz + 1) * EXT, :]

    def add_into(zz, start, size, ref):
        def step(i, _):
            at = pl.ds(mult(zz * ROWS + i * 32, 16), 32)
            where = cols(start, size)
            mine_out[at, where] = (
                mine_out[at, where].astype(F32) + ref(i)[...].astype(F32)
            ).astype(BF)
            return 0

        lax.fori_loop(0, ROWS // 32, step, 0)

    def add_cores(zz):
        drain(prcv.at[pl.ds(mult(zz * ROWS, 16), ROWS)], po_r.at[zz])
        add_into(zz, 0, HD, lambda i: prcv.at[pl.ds(mult(zz * ROWS + i * 32, 16), 32)])

    def sum_block(zz, n, s):
        return mine_out.at[pl.ds(mult(zz * ROWS, 16), ROWS), pl.ds(n * QD + s * XD, XD)]

    def r1_block(n, s):
        return r1.at[n, :, pl.ds(s * XD, XD)]

    def r2_block(side, n, s):
        return r2.at[side, :, pl.ds(n * QD + s * XD, XD)]

    def send_sum(src, dst, kind, s, dev):
        remote(src, dst, rs_s.at[2 * kind + s], rs_r.at[2 * kind + s], dev).start()

    def partials(k, _):
        zz = order(k)
        at = pl.ds(mult(zz * ROWS, 16), ROWS)

        @pl.when(k == 0)
        def _():
            drain(cot_block(zm, 0, QD), ag_r.at[0])
            ref = cot_block(zm, 0, QD)
            remote(ref, ref, agf_s.at[0], agf_r.at[0], up).start()
            drain(cot_block(zp, QD, QD), ag_r.at[3])
            ref2 = cot_block(zp, QD, QD)
            remote(ref2, ref2, agf_s.at[1], agf_r.at[1], down).start()

        drain(h.at[pl.ds(mult(zz * ROWS, 16), MAIN)], hm_r.at[zz])
        rows_in = h[at, :]

        def product(out, part):
            def tile(j, _):
                out[:, cols(j * QD, QD)] = dot(
                    rows_in, wv[:, cols(part * HD + j * QD, QD)]
                ).astype(BF)
                return 0

            lax.fori_loop(0, 2, tile, 0)

        product(other_out(zz), nc)
        remote(other_out(zz), prcv.at[at], po_s.at[zz], po_r.at[zz], sib).start()
        product(mine_out.at[at], c)

        @pl.when(k == 1)
        def _():
            add_cores(zo)
            for s in range(2):
                send_sum(sum_block(zo, 0, s), r1_block(0, s), 0, s, up)
                send_sum(sum_block(zo, 1, s), r1_block(1, s), 1, s, down)

        @pl.when(k == 2)
        def _():
            add_cores(zp)
            for s in range(2):
                send_sum(sum_block(zp, 1, s), r2_block(0, 1, s), 2, s, up)
            drain(cot_block(zm, QD, QD), ag_r.at[2])
            to_sibling(zm)
            drain(cot_block(zp, 0, QD), ag_r.at[1])
            to_sibling(zp)

        @pl.when(k == 3)
        def _():
            add_cores(zm)
            for s in range(2):
                send_sum(sum_block(zm, 0, s), r2_block(1, 0, s), 3, s, down)

        return 0

    lax.fori_loop(0, NZ, partials, 0)
    add_cores(z)

    def more_grads(k, _):
        zz = lax.rem(z + jnp.where(k == 0, 1, jnp.where(k == 1, 3, 2)), 4)

        @pl.when(k == 2)
        def _():
            drain(cot_block(zo, 0, QD), agf_r.at[0])
            drain(cot_block(zo, QD, QD), agf_r.at[1])
            to_sibling(zo)

        drain(other_half(zz), sib_r.at[zz])
        slot_grads(zz)
        return 0

    lax.fori_loop(0, 3, more_grads, 0)

    unswap = one(
        (iota((MAIN, MAIN), 1) // 64 == (iota((MAIN, MAIN), 0) // 4) % 4)
        & ((iota((MAIN, MAIN), 1) // 4) % 16 == iota((MAIN, MAIN), 0) // 16)
        & (iota((MAIN, MAIN), 1) % 4 == iota((MAIN, MAIN), 0) % 4)
    )
    drain(hp.at[pl.ds(0, 240)], hm_s.at[4])
    hpx[...] = sum(
        dot(unswap[:, zz * EXT : (zz + 1) * EXT], hp[zz * ROWS + MAIN : (zz + 1) * ROWS, :])
        for zz in range(NZ)
    ).astype(BF)
    send_slots(lambda p2: rows(hpx, p2 * 16, 16), rows(rx, p * 16, 16), ret_s.at[4], ret_r.at[4])

    for s in range(2):
        for n, zz, dev in ((0, zp, up), (1, zm, down)):
            drain(r1_block(n, s), rs_r.at[2 * n + s])
            add_into(
                zz,
                n * QD + s * XD,
                XD,
                lambda i: r1.at[n, pl.ds(mult(i * 32, 16), 32), pl.ds(s * XD, XD)],
            )
            send_sum(sum_block(zz, n, s), r2_block(n, n, s), 4 + n, s, dev)

    for zz in range(NZ):
        drain(prcv.at[0:ROWS], po_s.at[zz])

    def weight_grads(j, _):
        at = cols(j * XD, XD)
        wg[:, at] = dot_tn(h[...], cot[:, at]).astype(BF)
        return 0

    lax.fori_loop(0, 8, weight_grads, 0)

    drain(rx, ret_r.at[4])

    def tokens_grad(zz, _):
        at = pl.ds(mult(zz * MAIN, 16), MAIN)
        drain(rm.at[at], ret_r.at[zz])
        grads = dot_tn(table(zz), rm[at, :])
        late = dot_tn(extra_pick(zz, zz), rx[...])
        xh[pl.ds(mult(zz * MAIN, 16), TOK), :] = grads[0:TOK, :].astype(BF)
        xh[pl.ds(mult(zz * MAIN + TOK, 16), TOK), :] = (grads[TOK:, :] + late).astype(BF)
        return 0

    lax.fori_loop(0, NZ, tokens_grad, 0)

    for n in range(2):
        drain(half(gm, 0, 240, n), cm_s.at[n])
    drain(gx.at[pl.ds(0, 240)], cx_s.at[0])

    def return_grads(piece):
        for dc, dz in COLUMN:
            c2, z2, dev = column(dc, dz)
            src = rows(xh, (z2 * 2 + c2) * TOK + piece * 32, 32)
            dst = hg.at[pl.ds(mult(piece * 32, 16), 32), cols(blk * FB, FB)]
            remote(src, dst, hg_s.at[0], hg_r.at[0], dev).start()

    def last_sum(first, count, n, s):
        at = pl.ds(mult(z * ROWS + first, 16), count)
        there = pl.ds(mult(first, 16), count)
        where = pl.ds(n * QD + s * XD, XD)
        return (
            mine_out[at, where].astype(F32)
            + r2[0, there, where].astype(F32)
            + r2[1, there, where].astype(F32)
        ).astype(BF)

    back = (iota((MAIN, EXT), 1) // 4 == iota((MAIN, EXT), 0) // 16) & (
        iota((MAIN, EXT), 1) % 4 == iota((MAIN, EXT), 0) % 4
    )
    SD = XD // 2
    lax.fori_loop(0, 2, lambda piece, _: return_grads(piece) or 0, 0)
    for s in range(2):
        for kind, side, n in ((2, 0, 1), (3, 1, 0), (4, 0, 0), (5, 1, 1)):
            drain(r2_block(side, n, s), rs_r.at[2 * kind + s])
        if s == 1:
            lax.fori_loop(2, 4, lambda piece, _: return_grads(piece) or 0, 0)
        for n in range(2):

            def main_rows(i, _):
                at = pl.ds(mult(i * 32, 16), 32)
                gm[at, (2 * s + n) * XD : (2 * s + n + 1) * XD] = last_sum(i * 32, 32, n, s)
                return 0

            lax.fori_loop(0, MAIN // 32, main_rows, 0)
        send_slots(
            lambda p2: half(gm, p2 * 16, 16, s), half(em, p * 16, 16, s), eo_s.at[s], eo_r.at[s]
        )
        tails = [last_sum(MAIN, EXT, n, s) for n in range(2)]
        ex[:, s * SD : (s + 1) * SD] = sum(
            dot(
                one(back & ((iota((MAIN, EXT), 0) // 4) % 4 == q)),
                tails[q // 2][:, (q % 2) * SD : (q % 2 + 1) * SD],
            )
            for q in range(4)
        ).astype(BF)
        send_slots(
            lambda p2: ex.at[pl.ds(mult(p2 * 16, 16), 16), pl.ds(s * SD, SD)],
            exr.at[pl.ds(mult(p * 16, 16), 16), pl.ds(s * SD, SD)],
            eo_s.at[2 + s],
            eo_r.at[2 + s],
        )
    local(rows(xh, (z * 2 + c) * TOK, TOK), hg.at[:, cols(blk * FB, FB)], hg_r.at[0]).start()

    for s in range(2):
        drain(half(em, 0, MAIN, s), eo_r.at[s])
        drain(exr.at[:, pl.ds(s * SD, SD)], eo_r.at[2 + s])
        rows_out = dot_tn(table(z), em[:, s * QD : (s + 1) * QD])
        late = jnp.concatenate(
            [dot_tn(extra_pick(z, q), exr[:, s * SD : (s + 1) * SD]) for q in range(4)], axis=1
        )
        kk[0:TOK, s * QD : (s + 1) * QD] = rows_out[0:TOK, :].astype(BF)
        kk[TOK : 2 * TOK, s * QD : (s + 1) * QD] = (rows_out[TOK:, :] + late).astype(BF)
        src = kk.at[pl.ds(mult(nc * TOK, 16), TOK), pl.ds(s * QD, QD)]
        remote(src, kr.at[:, pl.ds(s * QD, QD)], k_s.at[s], k_r.at[s], sib).start()

    total = jnp.zeros((TOK, 1), F32)
    for core, ref, first in ((c, kk, mult(c * TOK, 16)), (nc, kr, 0)):
        for s in range(2):
            if ref is kr:
                drain(kr.at[:, pl.ds(s * QD, QD)], k_r.at[s])
            for n in range(2):
                at = cols(core * HD + n * QD + s * XD, XD)
                picked = ref[pl.ds(first, TOK), (2 * s + n) * XD : (2 * s + n + 1) * XD].astype(F32)
                total += jnp.sum(og[:, at].astype(F32) * picked, axis=1, keepdims=True)
                mixed[:, at] = (gate * picked).astype(BF)
    gg[...] = jnp.sum(jnp.where(eye, total, 0.0), axis=0, keepdims=True)

    for s in range(2):
        drain(kr.at[:, pl.ds(s * QD, QD)], k_s.at[s])
    drain(hg, hg_r.at[0])
    drain(rows(posv, 0, 56, 8), pos_s.at[0])
    drain(xh.at[pl.ds(0, 7 * TOK)], hg_s.at[0])
    drain(tsend, t_s.at[0])
    for s in range(2):
        drain(half(em, 0, 240, s), eo_s.at[s])
        drain(exr.at[pl.ds(0, 240), pl.ds(s * SD, SD)], eo_s.at[2 + s])
    for n in range(5):
        if n < 4:
            drain(hp.at[pl.ds(0, 240)], hm_s.at[n])
        drain(hp.at[pl.ds(0, 240)], ret_s.at[n])
    for n in range(4):
        drain(r1.at[0], ag_s.at[n])
        drain(r2.at[0], sib_s.at[n])
    for n in range(2):
        drain(r1.at[0], agf_s.at[n])
    for n in range(12):
        drain(r1_block(0, 0), rs_s.at[n])


PIECES = 4


def finish(mixed_in, hg_in, wg_in, gg_in, mixed, hg, wg, gg, sems):
    copies = [(mixed_in, mixed), (hg_in, hg), (gg_in, gg)]
    for k in range(PIECES):
        at = pl.ds(k * (FB // PIECES), FB // PIECES)
        copies.append((wg_in.at[at], wg.at[at]))
    copies = [pltpu.make_async_copy(a, b, sems.at[k]) for k, (a, b) in enumerate(copies)]
    for copy in copies:
        copy.start()
    for copy in copies:
        copy.wait()


def layer(hidden_in, weights, gates, group_ids, slot_ids, out_grad):
    vmem = pl.BlockSpec(memory_space=pltpu.VMEM)
    anywhere = pl.BlockSpec(memory_space=pl.ANY)
    sem = pltpu.SemaphoreType.DMA

    def buf(*shape):
        return pltpu.VMEM(shape, BF)

    gate_row = gates.reshape(1, TOK)
    results = pl.pallas_call(
        kernel,
        out_shape=(
            pltpu.VMEM((TOK, D), BF),
            pltpu.VMEM((TOK, FF), BF),
            pltpu.VMEM((FB, D), BF),
            pltpu.VMEM((1, TOK), F32),
        ),
        in_specs=[anywhere, anywhere, vmem, vmem, vmem, anywhere],
        out_specs=(vmem, vmem, vmem, vmem),
        scratch_shapes=[
            buf(FB, D),
            buf(NZ * ROWS, FB),
            buf(MAIN, FB),
            buf(NZ * ROWS, D),
            buf(MAIN, XD),
            buf(8 * TOK, FB),
            buf(NZ * MAIN, FB),
            buf(MAIN, FB),
            buf(2 * TOK, HD),
            buf(TOK, HD),
            buf(MAIN, HD),
            buf(MAIN, XD),
            buf(NZ * ROWS, HD),
            buf(NZ * ROWS, HD),
            buf(2, ROWS, QD),
            buf(2, ROWS, HD),
            buf(NZ * ROWS, FB),
            buf(NZ * MAIN, FB),
            buf(MAIN, FB),
            buf(TOK, HD),
            buf(TOK, D),
            buf(NZ * MAIN, 2 * TOK),
            buf(NZ * MAIN, TOK),
            pltpu.VMEM((8 * 8, TOK), jnp.int32),
            sem((1,)), sem((1,)),
            sem((1,)), sem((1,)),
            sem((1,)), sem((1,)), sem((1,)),
            sem((1,)), sem((1,)),
            sem((2,)), sem((2,)),
            sem((1,)), sem((1,)),
            sem((5,)), sem((5,)),
            sem((4,)), sem((4,)),
            sem((2,)), sem((2,)),
            sem((4,)), sem((4,)),
            sem((4,)), sem((4,)),
            sem((12,)), sem((12,)),
            sem((5,)), sem((5,)),
            sem((4,)), sem((4,)),
            sem((2,)), sem((2,)),
            sem((1,)), sem((1,)),
        ],
        compiler_params=pltpu.CompilerParams(
            collective_id=0, has_side_effects=True, vmem_limit_bytes=55104 * 1024
        ),
        cost_estimate=pl.CostEstimate(
            flops=6 * NZ * ROWS * FB * D, bytes_accessed=20_000_000, transcendentals=0
        ),
        name="experts",
    )(hidden_in, weights, gate_row, group_ids.reshape(1, TOK), slot_ids.reshape(1, TOK), out_grad)

    results = [pltpu.with_memory_space_constraint(value, pltpu.VMEM) for value in results]
    mixed, hidden_grad, weight_grad, gate_grad = pl.pallas_call(
        finish,
        out_shape=(
            jax.ShapeDtypeStruct((TOK, D), BF),
            jax.ShapeDtypeStruct((TOK, FF), BF),
            jax.ShapeDtypeStruct((FB, D), BF),
            jax.ShapeDtypeStruct((1, TOK), F32),
        ),
        in_specs=[vmem, vmem, vmem, vmem],
        out_specs=(anywhere, anywhere, anywhere, anywhere),
        scratch_shapes=[sem((PIECES + 3,))],
        compiler_params=pltpu.CompilerParams(vmem_limit_bytes=40 * 1024 * 1024),
        name="finish",
    )(*results)
    return mixed, hidden_grad, weight_grad, gate_grad.reshape(TOK)


def solution(mesh):
    wide, flat = P(("grp", "exp"), None), P(("grp", "exp"))
    return jax.shard_map(
        layer,
        mesh=mesh,
        in_specs=(wide, wide, flat, flat, flat, wide),
        out_specs=(wide, wide, wide, flat),
        check_vma=False,
    )
```
